512 devices in a mesh: query: 32 (over y, x, core), passage: 16 (over z).
Axes of the slice: x: 4, y: 4, z: 16, core: 2. Of those that a mesh axis runs over, the one named last changes fastest.
Arguments:
- queries: bfloat16 [4096, 4096], P('query'), may hold values from -12 to 12
- cand_ids: int32 [4096, 128], P('query'), may hold values from 0 to 2047, all different within a row
- teacher: int32 [4096, 128], P('query'), may hold values from 0 to 2047
- hidden_states: bfloat16 [2048, 4096], P('passage', 'query'), may hold values from -6 to 6
- gain: bfloat16 [4096], P('query'), may hold values from 0.5 to 1.5
Outputs:
- q_grad: bfloat16 [4096, 4096], P('query', 'passage')
- h_grad: bfloat16 [2048, 4096], P('passage', 'query')
- gain_grad: float32 [4096], P('query')
The draws below stay inside these ranges and needn't reach their ends.
Inputs may be any that keep to these rules, and one draw needn't show every extreme that they name: `cand_ids`: each query lists 128 different passages; every passage is listed by some query.
All inputs are finite; a program needn't handle non-finite values.
Results may differ from the reference program's by a relative error of at most 0.012.
The reference program's roundings to bfloat16 on the way (of `embedded`, `list_grad` and `grad_table`) count: a program that leaves them out, or rounds other values in their place, can miss the bound.
Values may be sent and summed in bfloat16 or wider, within the bound.
A program may use at most 64 MiB of HBM per device.

```python
import jax
import jax.numpy as jnp
from jax import lax

D = 4096
CAND = 128
NQ = 4096
NPASS = 2048


def draw_queries(key, part):
    key = jax.random.fold_in(key, 11)
    return jnp.clip(jax.random.normal(key, (NQ, D), jnp.float32), -6.0, 6.0).astype(jnp.bfloat16)


def draw_hidden_states(key, part):
    key = jax.random.fold_in(key, 23)
    return jnp.clip(jax.random.normal(key, (NPASS, D), jnp.float32), -6.0, 6.0).astype(jnp.bfloat16)


def with_ends(values, key, smallest, high):
    shape = values.shape
    place = [jax.random.randint(jax.random.fold_in(key, axis), (), 0, shape[axis]) for axis in range(len(shape))]
    values = values.at[tuple(place)].set(smallest)
    longest = shape.index(max(shape))
    place[longest] = (place[longest] + 1) % shape[longest]
    return values.at[tuple(place)].set(high)


def different_ones(key, rows, number_of, top, lift):
    ranking = jax.random.permutation(jax.random.fold_in(key, 1), number_of)
    boost = ranking
    for power in range(3):
        boost = boost * boost // number_of
    boost = boost * lift // number_of
    tickets = jax.random.randint(jax.random.fold_in(key, 2), (rows, number_of), 0, 4096) + boost
    fixed_rows = jax.random.permutation(jax.random.fold_in(key, 3), rows)[jnp.arange(number_of) % rows]
    tickets = jnp.where(jnp.arange(rows)[:, None] == fixed_rows[None, :], 1 << 14, tickets)
    priority = tickets * number_of + jnp.arange(number_of)
    return lax.top_k(priority.astype(jnp.int32), top)[1].astype(jnp.int32)


def setup_inputs(seed: int = 0) -> dict:
    seeds = jax.random.split(jax.random.key(seed), 6)
    queries = draw_queries(jax.random.fold_in(seeds[5], 71), 0)
    cand_ids = different_ones(seeds[1], NQ, NPASS, CAND, 1024)
    teacher = with_ends(jax.random.randint(seeds[2], (NQ, CAND), 0, 2048), jax.random.fold_in(seeds[2], 1), 0, 2047).astype(jnp.int32)
    hidden_states = draw_hidden_states(jax.random.fold_in(seeds[5], 71), 0)
    gain = jnp.clip(1.0 + 0.1 * jax.random.normal(seeds[4], (D,), jnp.float32), 0.5, 1.5).astype(jnp.bfloat16)
    return dict(queries=queries, cand_ids=cand_ids, teacher=teacher, hidden_states=hidden_states, gain=gain)


def reference(queries, cand_ids, teacher, hidden_states, gain):
    hidden_rows = hidden_states.astype(jnp.float32)
    inv_rms = lax.rsqrt(lax.optimization_barrier(jnp.mean(hidden_rows * hidden_rows, axis=1)) + 1e-05)
    gain_full = gain.astype(jnp.float32)
    embedded = (hidden_rows * inv_rms[:, None] * gain_full).astype(jnp.bfloat16)
    score_scale = float(D) ** (-0.5)
    dense_scores = jnp.dot(queries, embedded.T, preferred_element_type=jnp.float32) * score_scale
    scores = jnp.take_along_axis(dense_scores, cand_ids, axis=1)
    student = jax.nn.softmax(scores, axis=1)
    target = jax.nn.softmax(teacher.astype(jnp.float32) * 0.125, axis=1)
    list_grad = (student - target).astype(jnp.bfloat16)
    row_index = lax.broadcasted_iota(jnp.int32, cand_ids.shape, 0)
    grad_table = jnp.zeros((NQ, NPASS), jnp.bfloat16).at[row_index, cand_ids].set(list_grad)
    q_grad = jnp.dot(grad_table, embedded, preferred_element_type=jnp.float32).astype(jnp.bfloat16)
    e_grad = jnp.dot(grad_table.T, queries, preferred_element_type=jnp.float32)
    scaled = e_grad * gain_full
    row_mean = lax.optimization_barrier(jnp.mean(scaled * hidden_rows, axis=1))
    h_grad = (inv_rms[:, None] * scaled - hidden_rows * (inv_rms ** 3)[:, None] * row_mean[:, None]).astype(jnp.bfloat16)
    gain_grad = lax.optimization_barrier(jnp.sum(e_grad * hidden_rows * inv_rms[:, None], axis=0))
    return (q_grad, h_grad, gain_grad)
```

```python
import jax
import jax.numpy as jnp
from jax import lax
from jax.experimental import pallas as pl
from jax.experimental.pallas import tpu as pltpu
from jax.sharding import PartitionSpec as P

D = 4096
MESH = pl.DeviceIdType.MESH
F32, BF16, I32 = jnp.float32, jnp.bfloat16, jnp.int32
NZ = 16
NC = 16
B = 128
X = 144


def lanes(x, index):
    return jnp.take_along_axis(x, index, axis=1)


def kernel(
    q_ref, cand_ref, teach_ref, hid_ref, gain_ref,
    qg_ref, hg_ref, gg_ref,
    hf, hid32, xp, xz, ez, emb, inv, invp, tgt, tgt_t, sg, stat_s, stat_r, sp_s, sp_r,
    lg_s, lg_r, gfull, embz, eb, e32, sib_r, gs, gsib_r, gm_s, gm_r, s6_s, s6_r, z7_s, z7_r,
    s1_sem, s1_dir, s1_rel, small_sem, xz_sem, st_sem, sp_sem, lg_sem, ez_sem, ez_dir, ez_rel,
    sib_sem, gsib_sem, gm_sem, s6_sem, z7_sem,
):
    me = lax.axis_index("query")
    z = lax.axis_index("passage")
    core = lax.bitwise_and(me, 1)
    other = 1 - core
    chip = lax.shift_right_logical(me, 1)
    cy, cx = lax.shift_right_logical(chip, 2), lax.bitwise_and(chip, 3)
    sibling = {"query": 2 * chip + other}

    def chip_at(d):
        ty = lax.bitwise_and(cy + lax.shift_right_logical(d, 2), 3)
        tx = lax.bitwise_and(cx + d, 3)
        return 4 * ty + tx

    def z_at(d):
        return lax.bitwise_and(z + d, NZ - 1)

    def each(first, last, body):
        def step(d, carry):
            body(d)
            return carry

        lax.fori_loop(first, last, step, 0)

    def send(src, dst, s_sem, r_sem, where):
        pltpu.make_async_remote_copy(
            src_ref=src, dst_ref=dst, send_sem=s_sem, recv_sem=r_sem,
            device_id=where, device_id_type=MESH,
        ).start()

    def drain(ref, sem):
        pltpu.make_async_copy(ref, ref, sem).wait()

    barrier = pltpu.get_barrier_semaphore()

    def hail_z(d):
        pl.semaphore_signal(barrier, inc=1, device_id={"passage": z_at(d)}, device_id_type=MESH)

    def hail_plane(d):
        pl.semaphore_signal(
            barrier, inc=1, device_id={"query": lax.bitwise_and(me + d, 31)}, device_id_type=MESH
        )

    each(1, NZ, hail_z)
    each(1, 32, hail_plane)

    hid = hid_ref[...]
    gain_row = gain_ref[...].astype(F32)
    hf[core, chip, 0:B, :] = hid
    hf[core, chip, B:X, :] = jnp.broadcast_to(gain_row, (16, B)).astype(BF16)
    h32 = hid.astype(F32)
    hid32[...] = h32.reshape(NC, 8, B)
    xp[chip] = hid32[chip]

    t = teach_ref[...].astype(F32) * 0.125
    t = jnp.exp(t - jnp.max(t, axis=1, keepdims=True))
    tgt[...] = t / jnp.sum(t, axis=1, keepdims=True)

    lane = lax.broadcasted_iota(I32, (8, B), 1)
    owned_id = lane + z * B
    base = lax.shift_left(lax.shift_right_logical(lane, 3), 7) + lax.bitwise_and(lane, 7)

    def own_inverse(g):
        rows = pl.ds(pl.multiple_of(g * 8, 8), 8)
        cand = cand_ref[rows, :]
        acc = jnp.full((8, B), -1, I32)
        for c in range(B):
            acc = jnp.where(cand[:, c : c + 1] == owned_id, c, acc)
        invp[rows, :] = acc

    def full_inverse(g):
        rows = pl.ds(pl.multiple_of(g * 8, 8), 8)
        cand = cand_ref[rows, :]
        accs = [jnp.full((8, B), -1, I32) for _ in range(NC)]
        for c in range(B):
            one = jnp.broadcast_to(cand[:, c : c + 1], (8, B))
            for b in range(NC):
                accs[b] = jnp.where(one == base + 8 * b, c, accs[b])
        for b in range(NC):
            inv[rows, b * B : (b + 1) * B] = accs[b]

    each(0, 16, own_inverse)
    each(0, 8, full_inverse)

    pl.semaphore_wait(barrier, NZ - 1 + 31)

    def send_small(d):
        t = chip_at(d)
        send(hid32.at[t], xp.at[chip], small_sem.at[0], small_sem.at[1], {"query": 2 * t + core})

    def send_hidden(d):
        t = chip_at(d)
        block = hf.at[core, chip]
        send(block, block, s1_sem.at[0], s1_dir.at[chip], {"query": 2 * t + core})

    each(1, NC, send_small)
    own = hf.at[core, chip]
    send(own, own, s1_sem.at[1], s1_rel.at[0], sibling)
    each(1, NC, send_hidden)

    each(8, 16, full_inverse)

    drain(xp.at[pl.ds(0, NC - 1)], small_sem.at[1])
    xz[z] = xp[z]

    def send_slice(d):
        t = z_at(d)
        send(xp.at[t], xz.at[z], xz_sem.at[0], xz_sem.at[1], {"passage": t})

    each(1, NZ, send_slice)

    def relay_hidden(d):
        f = 4 * lax.bitwise_and(cy - lax.shift_right_logical(d, 2) + 4, 3) + lax.bitwise_and(cx - d + NC, 3)
        block = hf.at[core, f]
        drain(block, s1_dir.at[f])
        send(block, block, s1_sem.at[1], s1_rel.at[0], sibling)

    each(1, NC, relay_hidden)
    drain(hf.at[other], s1_rel.at[0])

    total = jnp.zeros((B, B), F32)
    for c in range(NC):
        for k in range(2):
            x = hf[k, c, 0:B, :].astype(F32)
            total = total + x * x
    inv_rms = lax.rsqrt(jnp.sum(total, axis=1, keepdims=True) / float(D) + 1e-05)
    for c in range(NC):
        for k in range(2):
            x = hf[k, c, 0:B, :].astype(F32)
            g = hf[k, c, B:X, :].astype(F32)[0:1, :]
            emb[:, (2 * c + k) * B : (2 * c + k + 1) * B] = (x * inv_rms * g).astype(BF16)
    scale = float(D) ** -0.5
    scores_t = (
        lax.dot_general(emb[...], q_ref[...], (((1,), (1,)), ((), ())), preferred_element_type=F32) * scale
    )
    inv_own = invp[...]
    listed = inv_own >= 0
    listed_t = listed.astype(F32).T > 0.0
    masked = jnp.where(listed_t, scores_t, -1e30)
    top = jnp.max(masked, axis=0, keepdims=True)
    weight = jnp.where(listed_t, jnp.exp(masked - top), 0.0)
    part = jnp.sum(weight, axis=0, keepdims=True)
    stat_s[0:1, :] = top
    stat_s[1:2, :] = part
    stat_r[z] = stat_s[...]

    def send_stat(d):
        send(stat_s, stat_r.at[z], st_sem.at[0], st_sem.at[1], {"passage": z_at(d)})

    each(1, NZ, send_stat)

    scores = scores_t.T
    for g in range(16):
        rows = slice(8 * g, 8 * g + 8)
        local = cand_ref[rows, :] - z * B
        mine = (local >= 0) & (local < B)
        sp_s[g] = jnp.where(mine, lanes(scores[rows, :], jnp.clip(local, 0, B - 1)), 0.0)
    sp_r[z] = sp_s[z]

    def send_sparse(d):
        t = z_at(d)
        send(sp_s.at[t], sp_r.at[z], sp_sem.at[0], sp_sem.at[1], {"passage": t})

    each(1, NZ, send_sparse)

    drain(xz.at[pl.ds(0, NZ - 1)], xz_sem.at[1])
    ez[core, chip] = xz[...].reshape(B, B).astype(BF16)

    def send_rows(d):
        t = chip_at(d)
        block = ez.at[core, chip]
        send(block, block, ez_sem.at[0], ez_dir.at[chip], {"query": 2 * t + core})

    own_rows = ez.at[core, chip]
    send(own_rows, own_rows, ez_sem.at[1], ez_rel.at[0], sibling)
    each(1, NC, send_rows)

    for g in range(16):
        rows = slice(8 * g, 8 * g + 8)
        i = inv_own[rows, :]
        sg[rows, :] = jnp.where(i >= 0, lanes(tgt[rows, :], jnp.maximum(i, 0)), 0.0)
    tgt_t[...] = sg[...].T

    drain(stat_r.at[pl.ds(0, NZ - 1)], st_sem.at[1])
    tops = [stat_r[k, 0:1, :] for k in range(NZ)]
    parts = [stat_r[k, 1:2, :] for k in range(NZ)]
    top_all = tops[0]
    for k in range(1, NZ):
        top_all = jnp.maximum(top_all, tops[k])
    norm = jnp.zeros((1, B), F32)
    for k in range(NZ):
        norm = norm + parts[k] * jnp.exp(tops[k] - top_all)
    table_t = jnp.where(listed_t, jnp.exp(masked - top_all) / norm - tgt_t[...], 0.0).astype(BF16)
    row_dot = jnp.sum(table_t.astype(F32) * scores_t, axis=1, keepdims=True)
    row_dot_row = jnp.broadcast_to(row_dot, (B, B)).T[0:1, :]
    for c in range(NC):
        both = jnp.dot(table_t, q_ref[:, c * 256 : (c + 1) * 256], preferred_element_type=F32)
        for k in range(2):
            e = both[:, k * B : (k + 1) * B]
            e32[k, c] = e
            eb[k, c] = e.astype(BF16)
            terms = e * hf[k, c, 0:B, :].astype(F32) * inv_rms
            gs[k, c, 0:1, :] = jnp.sum(terms, axis=0, keepdims=True)
            gs[k, c, 1:2, :] = row_dot_row
    send(gs.at[other], gsib_r, gsib_sem.at[0], gsib_sem.at[1], sibling)
    send(eb.at[other], sib_r, sib_sem.at[0], sib_sem.at[1], sibling)

    drain(sp_r.at[pl.ds(0, NZ - 1)], sp_sem.at[1])
    logits = sp_r[0]
    for k in range(1, NZ):
        logits = logits + sp_r[k]
    w = jnp.exp(logits - jnp.max(logits, axis=1, keepdims=True))
    student = w / jnp.sum(w, axis=1, keepdims=True)
    my_rows = pl.ds(pl.multiple_of(z * 8, 8), 8)
    lg_s[0:8, :] = (student - tgt[my_rows, :]).astype(BF16).astype(F32)
    lg_s[8:16, :] = jnp.broadcast_to(inv_rms, (B, B)).T[0:8, :]
    lg_r[z] = lg_s[...]

    def send_list(d):
        send(lg_s, lg_r.at[z], lg_sem.at[0], lg_sem.at[1], {"passage": z_at(d)})

    each(1, NZ, send_list)

    drain(gsib_r, gsib_sem.at[1])
    for c in range(NC):
        gm_s[c] = gs[core, c] + gsib_r[c]
    gm_r[chip] = gm_s[chip]

    def send_gain(d):
        t = chip_at(d)
        send(gm_s.at[t], gm_r.at[chip], gm_sem.at[0], gm_sem.at[1], {"query": 2 * t + core})

    each(1, NC, send_gain)
    drain(sib_r, sib_sem.at[1])
    for c in range(NC):
        s6_s[c] = (e32[core, c] + sib_r[c].astype(F32)).astype(BF16)
    s6_r[chip] = s6_s[chip]

    def send_grads(d):
        t = chip_at(d)
        send(s6_s.at[t], s6_r.at[chip], s6_sem.at[0], s6_sem.at[1], {"query": 2 * t + core})

    each(1, NC, send_grads)

    def relay_rows(d):
        f = 4 * lax.bitwise_and(cy - lax.shift_right_logical(d, 2) + 4, 3) + lax.bitwise_and(cx - d + NC, 3)
        block = ez.at[core, f]
        drain(block, ez_dir.at[f])
        send(block, block, ez_sem.at[1], ez_rel.at[0], sibling)

    each(1, NC, relay_rows)

    drain(gm_r.at[pl.ds(0, NC - 1)], gm_sem.at[1])
    small = gm_r[0]
    for c in range(1, NC):
        small = small + gm_r[c]
    z7_s[...] = small
    z7_r[z] = small

    def send_plane_gain(d):
        send(z7_s, z7_r.at[z], z7_sem.at[0], z7_sem.at[1], {"passage": z_at(d)})

    each(1, NZ, send_plane_gain)

    drain(lg_r.at[pl.ds(0, NZ - 1)], lg_sem.at[1])
    for g in range(0, 16, 2):
        for b in range(NC):
            cols = slice(b * B, (b + 1) * B)
            two = []
            for k in (g, g + 1):
                i = inv[8 * k : 8 * k + 8, cols]
                two.append(jnp.where(i >= 0, lanes(lg_r[k, 0:8, :], jnp.maximum(i, 0)), 0.0))
            gfull[8 * g : 8 * g + 16, cols] = jnp.concatenate(two, axis=0).astype(BF16)
    drain(ez.at[other], ez_rel.at[0])
    rms_rows = jnp.concatenate([lg_r[k, 8:9, :] for k in range(NZ)], axis=0)
    rms_t = jnp.concatenate([rms_rows, jnp.zeros((B - NZ, B), F32)], axis=0).T
    gains = [hf[k, z, B:X, :].astype(F32)[0:1, :] for k in range(2)]
    for c in range(NC):
        col = jnp.concatenate(
            [jnp.broadcast_to(rms_t[8 * c : 8 * c + 8, k : k + 1], (8, B)) for k in range(NZ)], axis=0
        )
        for k in range(2):
            raw = ez[k, c].astype(F32)
            embz[c * B : (c + 1) * B, k * B : (k + 1) * B] = (raw * col * gains[k]).astype(BF16)
    qg_ref[...] = jnp.dot(gfull[...], embz[...], preferred_element_type=F32).astype(BF16)

    drain(s6_r.at[pl.ds(0, NC - 1)], s6_sem.at[1])
    e_grad = s6_r[0].astype(F32)
    for c in range(1, NC):
        e_grad = e_grad + s6_r[c].astype(F32)
    dot_col = jnp.broadcast_to(small[1:2, :], (B, B)).T
    hg_ref[...] = (
        inv_rms * (e_grad * gain_row) - hid_ref[...].astype(F32) * (inv_rms * inv_rms) * (dot_col * scale)
    ).astype(BF16)

    drain(z7_r.at[pl.ds(0, NZ - 1)], z7_sem.at[1])
    gain_grad = z7_r[0, 0:1, :]
    for k in range(1, NZ):
        gain_grad = gain_grad + z7_r[k, 0:1, :]
    gg_ref[...] = gain_grad

    n = NC - 1
    drain(xp.at[pl.ds(0, n)], small_sem.at[0])
    drain(hf.at[0, pl.ds(0, n)], s1_sem.at[0])
    drain(hf.at[0], s1_sem.at[1])
    drain(xz.at[pl.ds(0, n)], xz_sem.at[0])
    drain(stat_r.at[pl.ds(0, n)], st_sem.at[0])
    drain(sp_r.at[pl.ds(0, n)], sp_sem.at[0])
    drain(lg_r.at[pl.ds(0, n)], lg_sem.at[0])
    drain(ez.at[0, pl.ds(0, n)], ez_sem.at[0])
    drain(ez.at[0], ez_sem.at[1])
    drain(gsib_r, gsib_sem.at[0])
    drain(sib_r, sib_sem.at[0])
    drain(gm_r.at[pl.ds(0, n)], gm_sem.at[0])
    drain(s6_r.at[pl.ds(0, n)], s6_sem.at[0])
    drain(z7_r.at[pl.ds(0, n)], z7_sem.at[0])


def shards(queries, cand_ids, teacher, hidden_states, gain):
    vmem = pl.BlockSpec(memory_space=pltpu.VMEM)
    two = pltpu.SemaphoreType.DMA((2,))
    q_grad, h_grad, gain_grad = pl.pallas_call(
        kernel,
        name="listwise",
        out_shape=(
            jax.ShapeDtypeStruct((B, 2 * B), BF16),
            jax.ShapeDtypeStruct((B, B), BF16),
            jax.ShapeDtypeStruct((1, B), F32),
        ),
        in_specs=[vmem] * 5,
        out_specs=(vmem, vmem, vmem),
        scratch_shapes=[
            pltpu.VMEM((2, NC, X, B), BF16),
            pltpu.VMEM((NC, 8, B), F32),
            pltpu.VMEM((NC, 8, B), F32),
            pltpu.VMEM((NZ, 8, B), F32),
            pltpu.VMEM((2, NC, B, B), BF16),
            pltpu.VMEM((B, D), BF16),
            pltpu.VMEM((B, NC * B), I32),
            pltpu.VMEM((B, B), I32),
            pltpu.VMEM((B, B), F32),
            pltpu.VMEM((B, B), F32),
            pltpu.VMEM((B, B), F32),
            pltpu.VMEM((8, B), F32),
            pltpu.VMEM((NZ, 8, B), F32),
            pltpu.VMEM((NZ, 8, B), F32),
            pltpu.VMEM((NZ, 8, B), F32),
            pltpu.VMEM((16, B), F32),
            pltpu.VMEM((NZ, 16, B), F32),
            pltpu.VMEM((B, NC * B), BF16),
            pltpu.VMEM((NC * B, 2 * B), BF16),
            pltpu.VMEM((2, NC, B, B), BF16),
            pltpu.VMEM((2, NC, B, B), F32),
            pltpu.VMEM((NC, B, B), BF16),
            pltpu.VMEM((2, NC, 8, B), F32),
            pltpu.VMEM((NC, 8, B), F32),
            pltpu.VMEM((NC, 8, B), F32),
            pltpu.VMEM((NC, 8, B), F32),
            pltpu.VMEM((NC, B, B), BF16),
            pltpu.VMEM((NC, B, B), BF16),
            pltpu.VMEM((8, B), F32),
            pltpu.VMEM((NZ, 8, B), F32),
            two,
            pltpu.SemaphoreType.DMA((NC,)),
            pltpu.SemaphoreType.DMA((1,)),
            two,
            two,
            two,
            two,
            two,
            two,
            pltpu.SemaphoreType.DMA((NC,)),
            pltpu.SemaphoreType.DMA((1,)),
            two,
            two,
            two,
            two,
            two,
        ],
        compiler_params=pltpu.CompilerParams(
            collective_id=0, has_side_effects=True, vmem_limit_bytes=48 * 2**20
        ),
    )(queries, cand_ids, teacher, hidden_states, gain.reshape(1, B))
    return q_grad, h_grad, gain_grad.reshape(B)


def solution(mesh):
    placed = (
        P("query", None),
        P("query", None),
        P("query", None),
        P("passage", "query"),
        P("query"),
    )
    return jax.shard_map(
        shards,
        mesh=mesh,
        in_specs=placed,
        out_specs=(P("query", "passage"), P("passage", "query"), P("query")),
        check_vma=False,
    )
```

```python
import jax
import jax.numpy as jnp
from jax import lax
from jax.experimental import pallas as pl
from jax.experimental.pallas import tpu as pltpu
from jax.sharding import PartitionSpec as P

D = 4096
MESH = pl.DeviceIdType.MESH
F32, BF16, I32 = jnp.float32, jnp.bfloat16, jnp.int32
FAR_FIRST = (10, 6, 9, 11, 14, 2, 8, 5, 7, 13, 15, 1, 3, 4, 12)
FAR_Z = (8, 7, 9, 6, 10, 5, 11, 4, 12, 3, 13, 2, 14, 1, 15)
NZ = 16
NC = 16
B = 128
X = 144


def lanes(x, index):
    return jnp.take_along_axis(x, index, axis=1)


def kernel(
    q_hbm, cand_hbm, teach_hbm, hid_hbm, gain_hbm,
    qg_ref, hg_ref, gg_ref,
    q_ref, cand_ref, teach_ref, hid_ref, gain_ref, in_sem,
    hf, hid32, xp, xz, ez, emb, inv, invp, tgt, tgt_t, sg, stat_s, stat_r, sp_s, sp_r,
    lg_s, lg_r, gfull, embz, eb, e32, sib_r, gs, gm_r, s6_s, s6_r, z7_s, z7_r,
    s1_sem, s1_dir, s1_rel, small_sem, xz_sem, st_sem, sp_sem, lg_sem, ez_sem, ez_dir, ez_rel,
    sib_sem, gm_sem, s6_sem, z7_sem,
):
    me = lax.axis_index("query")
    z = lax.axis_index("passage")
    core = lax.bitwise_and(me, 1)
    other = 1 - core
    chip = lax.shift_right_logical(me, 1)
    cy, cx = lax.shift_right_logical(chip, 2), lax.bitwise_and(chip, 3)
    sibling = {"query": 2 * chip + other}

    def chip_at(d):
        ty = lax.bitwise_and(cy + d // 4, 3)
        tx = lax.bitwise_and(cx + d, 3)
        return 4 * ty + tx

    def chip_from(d):
        return 4 * lax.bitwise_and(cy - d // 4 + 4, 3) + lax.bitwise_and(cx - d + NC, 3)

    def z_at(d):
        return lax.bitwise_and(z + d, NZ - 1)

    def plane_loop(body):
        for d in FAR_FIRST:
            body(d)

    def z_loop(body):
        for d in FAR_Z:
            body(d)

    def each(first, last, body):
        def step(d, carry):
            body(d)
            return carry

        lax.fori_loop(first, last, step, 0)

    def send(src, dst, s_sem, r_sem, where):
        pltpu.make_async_remote_copy(
            src_ref=src, dst_ref=dst, send_sem=s_sem, recv_sem=r_sem,
            device_id=where, device_id_type=MESH,
        ).start()

    def drain(ref, sem):
        pltpu.make_async_copy(ref, ref, sem).wait()

    arguments = [
        pltpu.make_async_copy(src, dst, in_sem.at[k])
        for k, (src, dst) in enumerate(
            [(hid_hbm, hid_ref), (gain_hbm, gain_ref), (cand_hbm, cand_ref), (teach_hbm, teach_ref), (q_hbm, q_ref)]
        )
    ]
    for argument in arguments:
        argument.start()

    barrier = pltpu.get_barrier_semaphore()

    def hail_z(d):
        pl.semaphore_signal(barrier, inc=1, device_id={"passage": z_at(d)}, device_id_type=MESH)

    def hail_plane(d):
        pl.semaphore_signal(
            barrier, inc=1, device_id={"query": lax.bitwise_and(me + d, 31)}, device_id_type=MESH
        )

    z_loop(hail_z)
    each(1, 32, hail_plane)

    arguments[0].wait()
    arguments[1].wait()
    hid = hid_ref[...]
    gain_row = gain_ref[...].astype(F32)
    hf[core, chip, 0:B, :] = hid
    hf[core, chip, B:X, :] = jnp.broadcast_to(gain_row, (16, B)).astype(BF16)
    h32 = hid.astype(F32)
    hid32[...] = h32.reshape(NC, 8, B)
    xp[chip] = hid32[chip]

    arguments[2].wait()
    arguments[3].wait()
    t = teach_ref[...].astype(F32) * 0.125
    t = jnp.exp(t - jnp.max(t, axis=1, keepdims=True))
    tgt[...] = t / jnp.sum(t, axis=1, keepdims=True)

    lane = lax.broadcasted_iota(I32, (8, B), 1)
    owned_id = lane + z * B
    base = lax.shift_left(lax.shift_right_logical(lane, 3), 7) + lax.bitwise_and(lane, 7)

    def own_inverse(g):
        rows = [pl.ds(pl.multiple_of(g * 32 + 8 * k, 8), 8) for k in range(4)]
        cands = [cand_ref[r, :] for r in rows]
        accs = [jnp.full((8, B), -1, I32) for _ in rows]
        for c in range(B):
            for k in range(4):
                accs[k] = jnp.where(cands[k][:, c : c + 1] == owned_id, c, accs[k])
        for k in range(4):
            invp[rows[k], :] = accs[k]

    def full_inverse(g):
        rows = pl.ds(pl.multiple_of(g * 8, 8), 8)
        cand = cand_ref[rows, :]
        accs = [jnp.full((8, B), -1, I32) for _ in range(NC)]
        for c in range(B):
            one = jnp.broadcast_to(cand[:, c : c + 1], (8, B))
            for b in range(NC):
                accs[b] = jnp.where(one == base + 8 * b, c, accs[b])
        for b in range(NC):
            inv[rows, b * B : (b + 1) * B] = accs[b]

    each(0, 4, own_inverse)

    pl.semaphore_wait(barrier, NZ - 1 + 31)

    def send_small(d):
        t = chip_at(d)
        send(hid32.at[t], xp.at[chip], small_sem.at[0], small_sem.at[1], {"query": 2 * t + core})

    def send_hidden(d):
        t = chip_at(d)
        block = hf.at[core, chip]
        send(block, block, s1_sem.at[0], s1_dir.at[chip], {"query": 2 * t + core})

    plane_loop(send_small)
    own = hf.at[core, chip]
    send(own, own, s1_sem.at[1], s1_rel.at[0], sibling)
    plane_loop(send_hidden)

    each(0, 4, full_inverse)

    drain(xp.at[pl.ds(0, NC - 1)], small_sem.at[1])
    xz[z] = xp[z]

    def send_slice(d):
        t = z_at(d)
        send(xp.at[t], xz.at[z], xz_sem.at[0], xz_sem.at[1], {"passage": t})

    z_loop(send_slice)

    def relay_hidden(d):
        f = chip_from(d)
        block = hf.at[core, f]
        drain(block, s1_dir.at[f])
        send(block, block, s1_sem.at[1], s1_rel.at[0], sibling)

    plane_loop(relay_hidden)
    drain(hf.at[other], s1_rel.at[0])

    total = jnp.zeros((B, B), F32)
    for c in range(NC):
        for k in range(2):
            x = hf[k, c, 0:B, :].astype(F32)
            total = total + x * x
    inv_rms = lax.rsqrt(jnp.sum(total, axis=1, keepdims=True) / float(D) + 1e-05)
    for c in range(NC):
        for k in range(2):
            x = hf[k, c, 0:B, :].astype(F32)
            g = hf[k, c, B:X, :].astype(F32)[0:1, :]
            emb[:, (2 * c + k) * B : (2 * c + k + 1) * B] = (x * inv_rms * g).astype(BF16)
    rms_row = jnp.broadcast_to(inv_rms, (B, B)).T[0:1, :]
    scale = float(D) ** -0.5
    arguments[4].wait()
    scores_t = (
        lax.dot_general(emb[...], q_ref[...], (((1,), (1,)), ((), ())), preferred_element_type=F32) * scale
    )
    inv_own = invp[...]
    listed = inv_own >= 0
    listed_t = listed.astype(F32).T > 0.0
    masked = jnp.where(listed_t, scores_t, -1e30)
    top = jnp.max(masked, axis=0, keepdims=True)
    weight = jnp.where(listed_t, jnp.exp(masked - top), 0.0)
    part = jnp.sum(weight, axis=0, keepdims=True)
    stat_s[0:1, :] = top
    stat_s[1:2, :] = part
    stat_s[2:3, :] = rms_row
    stat_r[z] = stat_s[...]

    def send_stat(d):
        send(stat_s, stat_r.at[z], st_sem.at[0], st_sem.at[1], {"passage": z_at(d)})

    z_loop(send_stat)

    scores = scores_t.T
    for g in range(16):
        rows = slice(8 * g, 8 * g + 8)
        local = cand_ref[rows, :] - z * B
        mine = (local >= 0) & (local < B)
        sp_s[g] = jnp.where(mine, lanes(scores[rows, :], jnp.clip(local, 0, B - 1)), 0.0)
    sp_r[z] = sp_s[z]

    def send_sparse(d):
        t = z_at(d)
        send(sp_s.at[t], sp_r.at[z], sp_sem.at[0], sp_sem.at[1], {"passage": t})

    z_loop(send_sparse)

    drain(xz.at[pl.ds(0, NZ - 1)], xz_sem.at[1])
    ez[core, chip] = xz[...].reshape(B, B).astype(BF16)

    def send_rows(d):
        t = chip_at(d)
        block = ez.at[core, chip]
        send(block, block, ez_sem.at[0], ez_dir.at[chip], {"query": 2 * t + core})

    own_rows = ez.at[core, chip]
    send(own_rows, own_rows, ez_sem.at[1], ez_rel.at[0], sibling)
    plane_loop(send_rows)

    for g in range(16):
        rows = slice(8 * g, 8 * g + 8)
        i = inv_own[rows, :]
        sg[rows, :] = jnp.where(i >= 0, lanes(tgt[rows, :], jnp.maximum(i, 0)), 0.0)
    tgt_t[...] = sg[...].T

    each(4, 12, full_inverse)

    drain(stat_r.at[pl.ds(0, NZ - 1)], st_sem.at[1])
    tops = [stat_r[k, 0:1, :] for k in range(NZ)]
    parts = [stat_r[k, 1:2, :] for k in range(NZ)]
    top_all = tops[0]
    for k in range(1, NZ):
        top_all = jnp.maximum(top_all, tops[k])
    norm = jnp.zeros((1, B), F32)
    for k in range(NZ):
        norm = norm + parts[k] * jnp.exp(tops[k] - top_all)
    table_t = jnp.where(listed_t, jnp.exp(masked - top_all) / norm - tgt_t[...], 0.0).astype(BF16)
    row_dot = jnp.sum(table_t.astype(F32) * scores_t, axis=1, keepdims=True)
    row_dot_row = jnp.broadcast_to(row_dot, (B, B)).T[0:1, :]
    for c in range(NC):
        both = jnp.dot(table_t, q_ref[:, c * 256 : (c + 1) * 256], preferred_element_type=F32)
        for k in range(2):
            e = both[:, k * B : (k + 1) * B]
            e32[k, c] = e
            eb[k, c] = e.astype(BF16)
            terms = e * hf[k, c, 0:B, :].astype(F32) * inv_rms
            gs[2 * c + k, 0:1, :] = jnp.sum(terms, axis=0, keepdims=True)
            gs[2 * c + k, 1:2, :] = row_dot_row
    gm_r[me] = gs[me]

    def send_gain(d):
        for k in (core, other):
            t = 2 * chip_at(d) + k
            send(gs.at[t], gm_r.at[me], gm_sem.at[0], gm_sem.at[1], {"query": t})

    plane_loop(send_gain)
    send(gs.at[2 * chip + other], gm_r.at[me], gm_sem.at[0], gm_sem.at[1], sibling)
    send(eb.at[other], sib_r, sib_sem.at[0], sib_sem.at[1], sibling)

    drain(sp_r.at[pl.ds(0, NZ - 1)], sp_sem.at[1])
    logits = sp_r[0]
    for k in range(1, NZ):
        logits = logits + sp_r[k]
    w = jnp.exp(logits - jnp.max(logits, axis=1, keepdims=True))
    student = w / jnp.sum(w, axis=1, keepdims=True)
    my_rows = pl.ds(pl.multiple_of(z * 8, 8), 8)
    lg_s[...] = (student - tgt[my_rows, :]).astype(BF16).astype(F32)
    lg_r[z] = lg_s[...]

    def send_list(d):
        send(lg_s, lg_r.at[z], lg_sem.at[0], lg_sem.at[1], {"passage": z_at(d)})

    z_loop(send_list)

    drain(sib_r, sib_sem.at[1])
    for c in range(NC):
        s6_s[c] = (e32[core, c] + sib_r[c].astype(F32)).astype(BF16)
    s6_r[chip] = s6_s[chip]

    def send_grads(d):
        t = chip_at(d)
        send(s6_s.at[t], s6_r.at[chip], s6_sem.at[0], s6_sem.at[1], {"query": 2 * t + core})

    plane_loop(send_grads)

    def relay_rows(d):
        f = chip_from(d)
        block = ez.at[core, f]
        drain(block, ez_dir.at[f])
        send(block, block, ez_sem.at[1], ez_rel.at[0], sibling)

    plane_loop(relay_rows)

    each(12, 16, full_inverse)

    drain(gm_r.at[pl.ds(0, 31)], gm_sem.at[1])
    small = gm_r[0]
    for k in range(1, 32):
        small = small + gm_r[k]
    z7_s[...] = small[0:1, :]
    z7_r[z] = small[0:1, :]

    def send_plane_gain(d):
        send(z7_s, z7_r.at[z], z7_sem.at[0], z7_sem.at[1], {"passage": z_at(d)})

    z_loop(send_plane_gain)

    drain(ez.at[other], ez_rel.at[0])
    rms_rows = jnp.concatenate([stat_r[k, 2:3, :] for k in range(NZ)], axis=0)
    rms_t = jnp.concatenate([rms_rows, jnp.zeros((B - NZ, B), F32)], axis=0).T
    gains = [hf[k, z, B:X, :].astype(F32)[0:1, :] for k in range(2)]
    for c in range(NC):
        col = jnp.concatenate(
            [jnp.broadcast_to(rms_t[8 * c : 8 * c + 8, k : k + 1], (8, B)) for k in range(NZ)], axis=0
        )
        for k in range(2):
            raw = ez[k, c].astype(F32)
            embz[c * B : (c + 1) * B, k * B : (k + 1) * B] = (raw * col * gains[k]).astype(BF16)
    drain(lg_r.at[pl.ds(0, NZ - 1)], lg_sem.at[1])
    for g in range(0, 16, 2):
        for b in range(NC):
            cols = slice(b * B, (b + 1) * B)
            two = []
            for k in (g, g + 1):
                i = inv[8 * k : 8 * k + 8, cols]
                two.append(jnp.where(i >= 0, lanes(lg_r[k], jnp.maximum(i, 0)), 0.0))
            gfull[8 * g : 8 * g + 16, cols] = jnp.concatenate(two, axis=0).astype(BF16)
    qg_ref[...] = jnp.dot(gfull[...], embz[...], preferred_element_type=F32).astype(BF16)

    drain(s6_r.at[pl.ds(0, NC - 1)], s6_sem.at[1])
    e_grad = s6_r[0].astype(F32)
    for c in range(1, NC):
        e_grad = e_grad + s6_r[c].astype(F32)
    dot_col = jnp.broadcast_to(small[1:2, :], (B, B)).T
    hg_ref[...] = (
        inv_rms * (e_grad * gain_row) - hid_ref[...].astype(F32) * (inv_rms * inv_rms) * (dot_col * scale)
    ).astype(BF16)

    drain(z7_r.at[pl.ds(0, NZ - 1)], z7_sem.at[1])
    gain_grad = z7_r[0]
    for k in range(1, NZ):
        gain_grad = gain_grad + z7_r[k]
    gg_ref[...] = gain_grad

    n = NC - 1
    drain(xp.at[pl.ds(0, n)], small_sem.at[0])
    drain(hf.at[0, pl.ds(0, n)], s1_sem.at[0])
    drain(hf.at[0], s1_sem.at[1])
    drain(xz.at[pl.ds(0, n)], xz_sem.at[0])
    drain(stat_r.at[pl.ds(0, n)], st_sem.at[0])
    drain(sp_r.at[pl.ds(0, n)], sp_sem.at[0])
    drain(lg_r.at[pl.ds(0, n)], lg_sem.at[0])
    drain(ez.at[0, pl.ds(0, n)], ez_sem.at[0])
    drain(ez.at[0], ez_sem.at[1])
    drain(sib_r, sib_sem.at[0])
    drain(gm_r.at[pl.ds(0, 31)], gm_sem.at[0])
    drain(s6_r.at[pl.ds(0, n)], s6_sem.at[0])
    drain(z7_r.at[pl.ds(0, n)], z7_sem.at[0])


def shards(queries, cand_ids, teacher, hidden_states, gain):
    vmem = pl.BlockSpec(memory_space=pltpu.VMEM)
    two = pltpu.SemaphoreType.DMA((2,))
    arguments = (queries, cand_ids, teacher, hidden_states, gain.reshape(1, B))
    q_grad, h_grad, gain_grad = pl.pallas_call(
        kernel,
        name="listwise",
        out_shape=(
            jax.ShapeDtypeStruct((B, 2 * B), BF16),
            jax.ShapeDtypeStruct((B, B), BF16),
            jax.ShapeDtypeStruct((1, B), F32),
        ),
        in_specs=[pl.BlockSpec(memory_space=pltpu.HBM)] * 5,
        out_specs=(vmem, vmem, vmem),
        scratch_shapes=[
            pltpu.VMEM((B, D), BF16),
            pltpu.VMEM((B, B), I32),
            pltpu.VMEM((B, B), I32),
            pltpu.VMEM((B, B), BF16),
            pltpu.VMEM((1, B), BF16),
            pltpu.SemaphoreType.DMA((5,)),
            pltpu.VMEM((2, NC, X, B), BF16),
            pltpu.VMEM((NC, 8, B), F32),
            pltpu.VMEM((NC, 8, B), F32),
            pltpu.VMEM((NZ, 8, B), F32),
            pltpu.VMEM((2, NC, B, B), BF16),
            pltpu.VMEM((B, D), BF16),
            pltpu.VMEM((B, NC * B), I32),
            pltpu.VMEM((B, B), I32),
            pltpu.VMEM((B, B), F32),
            pltpu.VMEM((B, B), F32),
            pltpu.VMEM((B, B), F32),
            pltpu.VMEM((4, B), F32),
            pltpu.VMEM((NZ, 4, B), F32),
            pltpu.VMEM((NZ, 8, B), F32),
            pltpu.VMEM((NZ, 8, B), F32),
            pltpu.VMEM((8, B), F32),
            pltpu.VMEM((NZ, 8, B), F32),
            pltpu.VMEM((B, NC * B), BF16),
            pltpu.VMEM((NC * B, 2 * B), BF16),
            pltpu.VMEM((2, NC, B, B), BF16),
            pltpu.VMEM((2, NC, B, B), F32),
            pltpu.VMEM((NC, B, B), BF16),
            pltpu.VMEM((32, 2, B), F32),
            pltpu.VMEM((32, 2, B), F32),
            pltpu.VMEM((NC, B, B), BF16),
            pltpu.VMEM((NC, B, B), BF16),
            pltpu.VMEM((1, B), F32),
            pltpu.VMEM((NZ, 1, B), F32),
            two,
            pltpu.SemaphoreType.DMA((NC,)),
            pltpu.SemaphoreType.DMA((1,)),
            two,
            two,
            two,
            two,
            two,
            two,
            pltpu.SemaphoreType.DMA((NC,)),
            pltpu.SemaphoreType.DMA((1,)),
            two,
            two,
            two,
            two,
        ],
        compiler_params=pltpu.CompilerParams(
            collective_id=0, has_side_effects=True, vmem_limit_bytes=48 * 2**20
        ),
    )(*[pltpu.with_memory_space_constraint(x, pltpu.HBM) for x in arguments])
    return q_grad, h_grad, gain_grad.reshape(B)


def solution(mesh):
    placed = (
        P("query", None),
        P("query", None),
        P("query", None),
        P("passage", "query"),
        P("query"),
    )
    return jax.shard_map(
        shards,
        mesh=mesh,
        in_specs=placed,
        out_specs=(P("query", "passage"), P("passage", "query"), P("query")),
        check_vma=False,
    )
```

```python
import jax
import jax.numpy as jnp
from jax import lax
from jax.experimental import pallas as pl
from jax.experimental.pallas import tpu as pltpu
from jax.sharding import PartitionSpec as P

D = 4096
MESH = pl.DeviceIdType.MESH
F32, BF16, I32 = jnp.float32, jnp.bfloat16, jnp.int32
FAR_FIRST = (10, 6, 9, 11, 14, 2, 8, 5, 7, 13, 15, 1, 3, 4, 12)
NEAR_Z = (4, 12, 3, 13, 2, 14, 1, 15)
FAR_Z = (8, 7, 9, 6, 10, 5, 11, 4, 12, 3, 13, 2, 14, 1, 15)
NZ = 16
NC = 16
B = 128
X = 144


def lanes(x, index):
    return jnp.take_along_axis(x, index, axis=1)


def kernel(
    q_hbm, cand_hbm, teach_hbm, hid_hbm, gain_hbm,
    qg_ref, hg_ref, gg_ref,
    q_ref, cand_ref, teach_ref, hid_ref, gain_ref, in_sem,
    hf, hid32, xp, xz, ez, emb, cand_t, inv_at, inv_code, inv_t, inv, tgt, tgt_t, sg, stat_s, stat_r, sp_s, sp_r,
    lg_s, lg_r, gfull, embz, eb, e32, sib_r, gs, gm_r, s6_s, s6_r, z7_s, z7_r,
    s1_sem, s1_dir, s1_rel, small_sem, xz_sem, st_sem, sp_sem, lg_sem, ez_sem, ez_dir, ez_rel,
    sib_sem, gm_sem, s6_sem, z7_sem, far_sem,
):
    me = lax.axis_index("query")
    z = lax.axis_index("passage")
    core = lax.bitwise_and(me, 1)
    other = 1 - core
    chip = lax.shift_right_logical(me, 1)
    cy, cx = lax.shift_right_logical(chip, 2), lax.bitwise_and(chip, 3)
    sibling = {"query": 2 * chip + other}

    def chip_at(d):
        ty = lax.bitwise_and(cy + d // 4, 3)
        tx = lax.bitwise_and(cx + d, 3)
        return 4 * ty + tx

    def chip_from(d):
        return 4 * lax.bitwise_and(cy - d // 4 + 4, 3) + lax.bitwise_and(cx - d + NC, 3)

    def z_at(d):
        return lax.bitwise_and(z + d, NZ - 1)

    def plane_loop(body):
        for d in FAR_FIRST:
            body(d)

    def z_loop(body):
        for d in FAR_Z:
            body(d)

    def each(first, last, body):
        def step(d, carry):
            body(d)
            return carry

        lax.fori_loop(first, last, step, 0)

    def send(src, dst, s_sem, r_sem, where):
        pltpu.make_async_remote_copy(
            src_ref=src, dst_ref=dst, send_sem=s_sem, recv_sem=r_sem,
            device_id=where, device_id_type=MESH,
        ).start()

    def drain(ref, sem):
        pltpu.make_async_copy(ref, ref, sem).wait()

    arguments = [
        pltpu.make_async_copy(src, dst, in_sem.at[k])
        for k, (src, dst) in enumerate(
            [(hid_hbm, hid_ref), (gain_hbm, gain_ref), (cand_hbm, cand_ref), (teach_hbm, teach_ref), (q_hbm, q_ref)]
        )
    ]
    for argument in arguments:
        argument.start()

    barrier = pltpu.get_barrier_semaphore()

    def hail_z(d):
        pl.semaphore_signal(barrier, inc=1, device_id={"passage": z_at(d)}, device_id_type=MESH)

    def hail_plane(d):
        pl.semaphore_signal(
            barrier, inc=1, device_id={"query": lax.bitwise_and(me + d, 31)}, device_id_type=MESH
        )

    for d in NEAR_Z:
        hail_z(d)
    each(1, 32, hail_plane)

    arguments[0].wait()
    arguments[1].wait()
    hid = hid_ref[...]
    gain_row = gain_ref[...].astype(F32)
    hf[core, chip, 0:B, :] = hid
    hf[core, chip, B:X, :] = jnp.broadcast_to(gain_row, (16, B)).astype(BF16)
    h32 = hid.astype(F32)
    hid32[...] = h32.reshape(NC, 8, B)
    xp[chip] = hid32[chip]

    arguments[2].wait()
    arguments[3].wait()
    t = teach_ref[...].astype(F32) * 0.125
    t = jnp.exp(t - jnp.max(t, axis=1, keepdims=True))
    tgt[...] = t / jnp.sum(t, axis=1, keepdims=True)

    cand_t[...] = cand_ref[...].T
    own_at = lax.broadcasted_iota(I32, (B, B), 0) + z * B

    def own_step(k, acc):
        for c in range(8):
            acc = jnp.where(cand_t[pl.ds(8 * k + c, 1), :] == own_at, 8 * k + c, acc)
        return acc

    inv_own_t = lax.fori_loop(0, B // 8, own_step, jnp.full((B, B), -1, I32))
    listed_t = inv_own_t >= 0
    inv_own = inv_own_t.T

    ids = cand_t[...]
    place = lax.bitwise_and(lax.shift_right_logical(ids, 3), NC - 1)
    inv_at[...] = lax.shift_left(lax.shift_right_logical(ids, 7), 3) + lax.bitwise_and(ids, 7)
    code = lax.shift_left(
        lax.broadcasted_iota(I32, (B, B), 0) + 1, 8 * lax.bitwise_and(place, 3)
    )
    for w in range(4):
        inv_code[w] = jnp.where(lax.shift_right_logical(place, 2) == w, code, 0)

    def half_inverse(h):
        half = B // 2
        at = lax.broadcasted_iota(I32, (half, B), 0) + half * h

        def step(k, accs):
            accs = list(accs)
            for u in range(8):
                row = pl.ds(8 * k + u, 1)
                hit = inv_at[row, :] == at
                for w in range(4):
                    accs[w] = lax.bitwise_or(jnp.where(hit, inv_code[w, row, :], 0), accs[w])
            return tuple(accs)

        accs = lax.fori_loop(0, B // 8, step, tuple(jnp.zeros((half, B), I32) for _ in range(4)))
        for w in range(4):
            inv_t[w, half * h : half * (h + 1), :] = accs[w]

    pl.semaphore_wait(barrier, 31 + len(NEAR_Z))
    for d in (4, 12):
        pl.semaphore_signal(far_sem, inc=1, device_id={"passage": z_at(d)}, device_id_type=MESH)

    def send_small(d):
        t = chip_at(d)
        send(hid32.at[t], xp.at[chip], small_sem.at[0], small_sem.at[1], {"query": 2 * t + core})

    def send_hidden(d):
        t = chip_at(d)
        block = hf.at[core, chip]
        send(block, block, s1_sem.at[0], s1_dir.at[chip], {"query": 2 * t + core})

    plane_loop(send_small)
    own = hf.at[core, chip]
    send(own, own, s1_sem.at[1], s1_rel.at[0], sibling)
    plane_loop(send_hidden)

    half_inverse(0)

    pl.semaphore_wait(far_sem, 2)

    drain(xp.at[pl.ds(0, NC - 1)], small_sem.at[1])
    xz[z] = xp[z]

    def send_slice(d):
        t = z_at(d)
        send(xp.at[t], xz.at[z], xz_sem.at[0], xz_sem.at[1], {"passage": t})

    z_loop(send_slice)

    def relay_hidden(d):
        f = chip_from(d)
        block = hf.at[core, f]
        drain(block, s1_dir.at[f])
        send(block, block, s1_sem.at[1], s1_rel.at[0], sibling)

    plane_loop(relay_hidden)
    drain(hf.at[other], s1_rel.at[0])

    total = jnp.zeros((B, B), F32)
    for c in range(NC):
        for k in range(2):
            x = hf[k, c, 0:B, :].astype(F32)
            total = total + x * x
    inv_rms = lax.rsqrt(jnp.sum(total, axis=1, keepdims=True) / float(D) + 1e-05)
    for c in range(NC):
        for k in range(2):
            x = hf[k, c, 0:B, :].astype(F32)
            g = hf[k, c, B:X, :].astype(F32)[0:1, :]
            emb[:, (2 * c + k) * B : (2 * c + k + 1) * B] = (x * inv_rms * g).astype(BF16)
    rms_row = jnp.broadcast_to(inv_rms, (B, B)).T[0:1, :]
    scale = float(D) ** -0.5
    arguments[4].wait()
    scores_t = (
        lax.dot_general(emb[...], q_ref[...], (((1,), (1,)), ((), ())), preferred_element_type=F32) * scale
    )
    masked = jnp.where(listed_t, scores_t, -1e30)
    top = jnp.max(masked, axis=0, keepdims=True)
    weight = jnp.where(listed_t, jnp.exp(masked - top), 0.0)
    part = jnp.sum(weight, axis=0, keepdims=True)
    stat_s[0:1, :] = top
    stat_s[1:2, :] = part
    stat_s[2:3, :] = rms_row
    stat_r[z] = stat_s[...]

    def send_stat(d):
        send(stat_s, stat_r.at[z], st_sem.at[0], st_sem.at[1], {"passage": z_at(d)})

    z_loop(send_stat)

    scores = scores_t.T
    for g in range(16):
        rows = slice(8 * g, 8 * g + 8)
        local = cand_ref[rows, :] - z * B
        mine = (local >= 0) & (local < B)
        sp_s[g] = jnp.where(mine, lanes(scores[rows, :], jnp.clip(local, 0, B - 1)), 0.0)
    sp_r[z] = sp_s[z]

    def send_sparse(d):
        t = z_at(d)
        send(sp_s.at[t], sp_r.at[z], sp_sem.at[0], sp_sem.at[1], {"passage": t})

    z_loop(send_sparse)

    for g in range(16):
        rows = slice(8 * g, 8 * g + 8)
        i = inv_own[rows, :]
        sg[rows, :] = jnp.where(i >= 0, lanes(tgt[rows, :], jnp.maximum(i, 0)), 0.0)
    tgt_t[...] = sg[...].T

    half_inverse(1)
    for w in range(4):
        inv[w] = inv_t[w].T

    drain(xz.at[pl.ds(0, NZ - 1)], xz_sem.at[1])
    ez[core, chip] = xz[...].reshape(B, B).astype(BF16)

    def send_rows(d):
        t = chip_at(d)
        block = ez.at[core, chip]
        send(block, block, ez_sem.at[0], ez_dir.at[chip], {"query": 2 * t + core})

    own_rows = ez.at[core, chip]
    send(own_rows, own_rows, ez_sem.at[1], ez_rel.at[0], sibling)
    plane_loop(send_rows)

    drain(stat_r.at[pl.ds(0, NZ - 1)], st_sem.at[1])
    tops = [stat_r[k, 0:1, :] for k in range(NZ)]
    parts = [stat_r[k, 1:2, :] for k in range(NZ)]
    top_all = tops[0]
    for k in range(1, NZ):
        top_all = jnp.maximum(top_all, tops[k])
    norm = jnp.zeros((1, B), F32)
    for k in range(NZ):
        norm = norm + parts[k] * jnp.exp(tops[k] - top_all)
    table_t = jnp.where(listed_t, jnp.exp(masked - top_all) / norm - tgt_t[...], 0.0).astype(BF16)
    row_dot = jnp.sum(table_t.astype(F32) * scores_t, axis=1, keepdims=True)
    row_dot_row = jnp.broadcast_to(row_dot, (B, B)).T[0:1, :]
    for c in range(NC):
        both = jnp.dot(table_t, q_ref[:, c * 256 : (c + 1) * 256], preferred_element_type=F32)
        for k in range(2):
            e = both[:, k * B : (k + 1) * B]
            e32[k, c] = e
            eb[k, c] = e.astype(BF16)
            terms = e * hf[k, c, 0:B, :].astype(F32) * inv_rms
            gs[2 * c + k, 0:1, :] = jnp.sum(terms, axis=0, keepdims=True)
            gs[2 * c + k, 1:2, :] = row_dot_row
    gm_r[me] = gs[me]

    def send_gain(d):
        for k in (core, other):
            t = 2 * chip_at(d) + k
            send(gs.at[t], gm_r.at[me], gm_sem.at[0], gm_sem.at[1], {"query": t})

    plane_loop(send_gain)
    send(gs.at[2 * chip + other], gm_r.at[me], gm_sem.at[0], gm_sem.at[1], sibling)
    send(eb.at[other], sib_r, sib_sem.at[0], sib_sem.at[1], sibling)

    drain(sp_r.at[pl.ds(0, NZ - 1)], sp_sem.at[1])
    logits = sp_r[0]
    for k in range(1, NZ):
        logits = logits + sp_r[k]
    w = jnp.exp(logits - jnp.max(logits, axis=1, keepdims=True))
    student = w / jnp.sum(w, axis=1, keepdims=True)
    my_rows = pl.ds(pl.multiple_of(z * 8, 8), 8)
    lg_s[...] = (student - tgt[my_rows, :]).astype(BF16).astype(F32)
    lg_r[z] = lg_s[...]

    def send_list(d):
        send(lg_s, lg_r.at[z], lg_sem.at[0], lg_sem.at[1], {"passage": z_at(d)})

    z_loop(send_list)

    drain(sib_r, sib_sem.at[1])
    for c in range(NC):
        s6_s[c] = (e32[core, c] + sib_r[c].astype(F32)).astype(BF16)
    s6_r[chip] = s6_s[chip]

    def send_grads(d):
        t = chip_at(d)
        send(s6_s.at[t], s6_r.at[chip], s6_sem.at[0], s6_sem.at[1], {"query": 2 * t + core})

    plane_loop(send_grads)

    drain(gm_r.at[pl.ds(0, 31)], gm_sem.at[1])
    small = gm_r[0]
    for k in range(1, 32):
        small = small + gm_r[k]
    z7_s[...] = small[0:1, :]
    z7_r[z] = small[0:1, :]

    def send_plane_gain(d):
        send(z7_s, z7_r.at[z], z7_sem.at[0], z7_sem.at[1], {"passage": z_at(d)})

    z_loop(send_plane_gain)

    def relay_rows(d):
        f = chip_from(d)
        block = ez.at[core, f]
        drain(block, ez_dir.at[f])
        send(block, block, ez_sem.at[1], ez_rel.at[0], sibling)

    plane_loop(relay_rows)


    drain(ez.at[other], ez_rel.at[0])
    rms_rows = jnp.concatenate([stat_r[k, 2:3, :] for k in range(NZ)], axis=0)
    rms_t = jnp.concatenate([rms_rows, jnp.zeros((B - NZ, B), F32)], axis=0).T
    gains = [hf[k, z, B:X, :].astype(F32)[0:1, :] for k in range(2)]
    for c in range(NC):
        col = jnp.concatenate(
            [jnp.broadcast_to(rms_t[8 * c : 8 * c + 8, k : k + 1], (8, B)) for k in range(NZ)], axis=0
        )
        for k in range(2):
            raw = ez[k, c].astype(F32)
            embz[c * B : (c + 1) * B, k * B : (k + 1) * B] = (raw * col * gains[k]).astype(BF16)
    drain(lg_r.at[pl.ds(0, NZ - 1)], lg_sem.at[1])
    for g in range(0, 16, 2):
        for b in range(NC):
            cols = slice(b * B, (b + 1) * B)
            two = []
            for k in (g, g + 1):
                i = lax.shift_right_logical(inv[b // 4, 8 * k : 8 * k + 8, :], 8 * (b % 4))
                i = lax.bitwise_and(i, 255)
                two.append(jnp.where(i > 0, lanes(lg_r[k], jnp.maximum(i - 1, 0)), 0.0))
            gfull[8 * g : 8 * g + 16, cols] = jnp.concatenate(two, axis=0).astype(BF16)
    qg_ref[...] = jnp.dot(gfull[...], embz[...], preferred_element_type=F32).astype(BF16)

    drain(s6_r.at[pl.ds(0, NC - 1)], s6_sem.at[1])
    e_grad = s6_r[0].astype(F32)
    for c in range(1, NC):
        e_grad = e_grad + s6_r[c].astype(F32)
    dot_col = jnp.broadcast_to(small[1:2, :], (B, B)).T
    hg_ref[...] = (
        inv_rms * (e_grad * gain_row) - hid_ref[...].astype(F32) * (inv_rms * inv_rms) * (dot_col * scale)
    ).astype(BF16)

    drain(z7_r.at[pl.ds(0, NZ - 1)], z7_sem.at[1])
    gain_grad = z7_r[0]
    for k in range(1, NZ):
        gain_grad = gain_grad + z7_r[k]
    gg_ref[...] = gain_grad

    n = NC - 1
    drain(xp.at[pl.ds(0, n)], small_sem.at[0])
    drain(hf.at[0, pl.ds(0, n)], s1_sem.at[0])
    drain(hf.at[0], s1_sem.at[1])
    drain(xz.at[pl.ds(0, n)], xz_sem.at[0])
    drain(stat_r.at[pl.ds(0, n)], st_sem.at[0])
    drain(sp_r.at[pl.ds(0, n)], sp_sem.at[0])
    drain(lg_r.at[pl.ds(0, n)], lg_sem.at[0])
    drain(ez.at[0, pl.ds(0, n)], ez_sem.at[0])
    drain(ez.at[0], ez_sem.at[1])
    drain(sib_r, sib_sem.at[0])
    drain(gm_r.at[pl.ds(0, 31)], gm_sem.at[0])
    drain(s6_r.at[pl.ds(0, n)], s6_sem.at[0])
    drain(z7_r.at[pl.ds(0, n)], z7_sem.at[0])


def shards(queries, cand_ids, teacher, hidden_states, gain):
    vmem = pl.BlockSpec(memory_space=pltpu.VMEM)
    two = pltpu.SemaphoreType.DMA((2,))
    arguments = (queries, cand_ids, teacher, hidden_states, gain.reshape(1, B))
    q_grad, h_grad, gain_grad = pl.pallas_call(
        kernel,
        name="listwise",
        out_shape=(
            jax.ShapeDtypeStruct((B, 2 * B), BF16),
            jax.ShapeDtypeStruct((B, B), BF16),
            jax.ShapeDtypeStruct((1, B), F32),
        ),
        in_specs=[pl.BlockSpec(memory_space=pltpu.HBM)] * 5,
        out_specs=(vmem, vmem, vmem),
        scratch_shapes=[
            pltpu.VMEM((B, D), BF16),
            pltpu.VMEM((B, B), I32),
            pltpu.VMEM((B, B), I32),
            pltpu.VMEM((B, B), BF16),
            pltpu.VMEM((1, B), BF16),
            pltpu.SemaphoreType.DMA((5,)),
            pltpu.VMEM((2, NC, X, B), BF16),
            pltpu.VMEM((NC, 8, B), F32),
            pltpu.VMEM((NC, 8, B), F32),
            pltpu.VMEM((NZ, 8, B), F32),
            pltpu.VMEM((2, NC, B, B), BF16),
            pltpu.VMEM((B, D), BF16),
            pltpu.VMEM((B, B), I32),
            pltpu.VMEM((B, B), I32),
            pltpu.VMEM((4, B, B), I32),
            pltpu.VMEM((4, B, B), I32),
            pltpu.VMEM((4, B, B), I32),
            pltpu.VMEM((B, B), F32),
            pltpu.VMEM((B, B), F32),
            pltpu.VMEM((B, B), F32),
            pltpu.VMEM((4, B), F32),
            pltpu.VMEM((NZ, 4, B), F32),
            pltpu.VMEM((NZ, 8, B), F32),
            pltpu.VMEM((NZ, 8, B), F32),
            pltpu.VMEM((8, B), F32),
            pltpu.VMEM((NZ, 8, B), F32),
            pltpu.VMEM((B, NC * B), BF16),
            pltpu.VMEM((NC * B, 2 * B), BF16),
            pltpu.VMEM((2, NC, B, B), BF16),
            pltpu.VMEM((2, NC, B, B), F32),
            pltpu.VMEM((NC, B, B), BF16),
            pltpu.VMEM((32, 2, B), F32),
            pltpu.VMEM((32, 2, B), F32),
            pltpu.VMEM((NC, B, B), BF16),
            pltpu.VMEM((NC, B, B), BF16),
            pltpu.VMEM((1, B), F32),
            pltpu.VMEM((NZ, 1, B), F32),
            two,
            pltpu.SemaphoreType.DMA((NC,)),
            pltpu.SemaphoreType.DMA((1,)),
            two,
            two,
            two,
            two,
            two,
            two,
            pltpu.SemaphoreType.DMA((NC,)),
            pltpu.SemaphoreType.DMA((1,)),
            two,
            two,
            two,
            two,
            pltpu.SemaphoreType.REGULAR,
        ],
        compiler_params=pltpu.CompilerParams(
            collective_id=0, has_side_effects=True, vmem_limit_bytes=48 * 2**20
        ),
    )(*[pltpu.with_memory_space_constraint(x, pltpu.HBM) for x in arguments])
    return q_grad, h_grad, gain_grad.reshape(B)


def solution(mesh):
    placed = (
        P("query", None),
        P("query", None),
        P("query", None),
        P("passage", "query"),
        P("query"),
    )
    return jax.shard_map(
        shards,
        mesh=mesh,
        in_specs=placed,
        out_specs=(P("query", "passage"), P("passage", "query"), P("query")),
        check_vma=False,
    )
```

```python
import jax
import jax.numpy as jnp
from jax import lax
from jax.experimental import pallas as pl
from jax.experimental.pallas import tpu as pltpu
from jax.sharding import PartitionSpec as P

D = 4096
MESH = pl.DeviceIdType.MESH
F32, BF16, I32 = jnp.float32, jnp.bfloat16, jnp.int32
FAR_FIRST = (10, 6, 9, 11, 14, 2, 8, 5, 7, 13, 15, 1, 3, 4, 12)
NEAR_Z = (4, 12, 3, 13, 2, 14, 1, 15)
FAR_Z = (8, 7, 9, 6, 10, 5, 11, 4, 12, 3, 13, 2, 14, 1, 15)
NZ = 16
NC = 16
B = 128


def lanes(x, index):
    return jnp.take_along_axis(x, index, axis=1)


def kernel(
    q_hbm, cand_hbm, teach_hbm, hid_hbm, gain_hbm,
    qg_ref, hg_ref, gg_ref,
    q_ref, cand_ref, teach_ref, hid_ref, gain_ref, in_sem,
    hf, gains, gain_sem, gain_rel, hid32, xp, xz, ez, emb, cand_t, inv_at, inv_code, inv_t, inv, tgt, tgt_t, sg, stat_s, stat_r, sp_s, sp_r,
    lg_s, lg_r, gfull, embz, eb, e32, sib_r, gs, gm_r, s6_s, s6_r, z7_s, z7_r,
    s1_sem, s1_dir, s1_rel, small_sem, xz_sem, st_sem, sp_sem, lg_sem, ez_sem, ez_dir, ez_rel,
    sib_sem, gm_sem, s6_sem, z7_sem, far_sem,
):
    me = lax.axis_index("query")
    z = lax.axis_index("passage")
    core = lax.bitwise_and(me, 1)
    other = 1 - core
    chip = lax.shift_right_logical(me, 1)
    cy, cx = lax.shift_right_logical(chip, 2), lax.bitwise_and(chip, 3)
    sibling = {"query": 2 * chip + other}

    def chip_at(d):
        ty = lax.bitwise_and(cy + d // 4, 3)
        tx = lax.bitwise_and(cx + d, 3)
        return 4 * ty + tx

    def chip_from(d):
        return 4 * lax.bitwise_and(cy - d // 4 + 4, 3) + lax.bitwise_and(cx - d + NC, 3)

    def z_at(d):
        return lax.bitwise_and(z + d, NZ - 1)

    def plane_loop(body):
        for d in FAR_FIRST:
            body(d)

    def z_loop(body):
        for d in FAR_Z:
            body(d)

    def each(first, last, body):
        def step(d, carry):
            body(d)
            return carry

        lax.fori_loop(first, last, step, 0)

    def send(src, dst, s_sem, r_sem, where):
        pltpu.make_async_remote_copy(
            src_ref=src, dst_ref=dst, send_sem=s_sem, recv_sem=r_sem,
            device_id=where, device_id_type=MESH,
        ).start()

    def drain(ref, sem):
        pltpu.make_async_copy(ref, ref, sem).wait()

    arguments = [
        pltpu.make_async_copy(src, dst, in_sem.at[k])
        for k, (src, dst) in enumerate(
            [(hid_hbm, hid_ref), (gain_hbm, gain_ref), (cand_hbm, cand_ref), (teach_hbm, teach_ref), (q_hbm, q_ref)]
        )
    ]
    for argument in arguments:
        argument.start()

    barrier = pltpu.get_barrier_semaphore()

    def hail_z(d):
        pl.semaphore_signal(barrier, inc=1, device_id={"passage": z_at(d)}, device_id_type=MESH)

    def hail_plane(d):
        for k in (core, other):
            pl.semaphore_signal(barrier, inc=1, device_id={"query": 2 * chip_at(d) + k}, device_id_type=MESH)

    for d in NEAR_Z:
        hail_z(d)
    plane_loop(hail_plane)
    pl.semaphore_signal(barrier, inc=1, device_id=sibling, device_id_type=MESH)

    arguments[0].wait()
    arguments[1].wait()
    hid = hid_ref[...]
    gain_row = gain_ref[...].astype(F32)
    hf[core, chip] = hid
    gains[core, chip] = gain_row
    h32 = hid.astype(F32)
    hid32[...] = h32.reshape(NC, 8, B)
    xp[chip] = hid32[chip]

    arguments[2].wait()
    arguments[3].wait()
    t = teach_ref[...].astype(F32) * 0.125
    t = jnp.exp(t - jnp.max(t, axis=1, keepdims=True))
    tgt[...] = t / jnp.sum(t, axis=1, keepdims=True)

    cand_t[...] = cand_ref[...].T
    own_at = lax.broadcasted_iota(I32, (B, B), 0) + z * B

    def own_step(k, acc):
        for c in range(8):
            acc = jnp.where(cand_t[pl.ds(8 * k + c, 1), :] == own_at, 8 * k + c, acc)
        return acc

    inv_own_t = lax.fori_loop(0, B // 8, own_step, jnp.full((B, B), -1, I32))
    listed_t = inv_own_t >= 0
    inv_own = inv_own_t.T

    ids = cand_t[...]
    place = lax.bitwise_and(lax.shift_right_logical(ids, 3), NC - 1)
    inv_at[...] = lax.shift_left(lax.shift_right_logical(ids, 7), 3) + lax.bitwise_and(ids, 7)
    code = lax.shift_left(
        lax.broadcasted_iota(I32, (B, B), 0) + 1, 8 * lax.bitwise_and(place, 3)
    )
    for w in range(4):
        inv_code[w] = jnp.where(lax.shift_right_logical(place, 2) == w, code, 0)

    def half_inverse(h):
        half = B // 2
        at = lax.broadcasted_iota(I32, (half, B), 0) + half * h

        def step(k, accs):
            accs = list(accs)
            for u in range(8):
                row = pl.ds(8 * k + u, 1)
                hit = inv_at[row, :] == at
                for w in range(4):
                    accs[w] = lax.bitwise_or(jnp.where(hit, inv_code[w, row, :], 0), accs[w])
            return tuple(accs)

        accs = lax.fori_loop(0, B // 8, step, tuple(jnp.zeros((half, B), I32) for _ in range(4)))
        for w in range(4):
            inv_t[w, half * h : half * (h + 1), :] = accs[w]

    pl.semaphore_wait(barrier, 31 + len(NEAR_Z))
    for d in (4, 12):
        pl.semaphore_signal(far_sem, inc=1, device_id={"passage": z_at(d)}, device_id_type=MESH)

    def send_small(d):
        t = chip_at(d)
        send(hid32.at[t], xp.at[chip], small_sem.at[0], small_sem.at[1], {"query": 2 * t + core})

    def send_hidden(d):
        t = chip_at(d)
        block = hf.at[core, chip]
        send(block, block, s1_sem.at[0], s1_dir.at[chip], {"query": 2 * t + core})

    plane_loop(send_small)

    def send_own_gain(d):
        t = chip_at(d)
        row = gains.at[core, chip]
        send(row, row, gain_sem.at[0], gain_sem.at[1], {"query": 2 * t + core})

    plane_loop(send_own_gain)
    own = hf.at[core, chip]
    send(own, own, s1_sem.at[1], s1_rel.at[0], sibling)
    plane_loop(send_hidden)

    for g in range(16):
        rows = slice(8 * g, 8 * g + 8)
        i = inv_own[rows, :]
        sg[rows, :] = jnp.where(i >= 0, lanes(tgt[rows, :], jnp.maximum(i, 0)), 0.0)
    tgt_t[...] = sg[...].T
    half_inverse(0)

    pl.semaphore_wait(far_sem, 2)

    drain(xp.at[pl.ds(0, NC - 1)], small_sem.at[1])
    xz[z] = xp[z]

    def send_slice(d):
        t = z_at(d)
        send(xp.at[t], xz.at[z], xz_sem.at[0], xz_sem.at[1], {"passage": t})

    z_loop(send_slice)
    drain(gains.at[core, pl.ds(0, NC - 1)], gain_sem.at[1])
    send(gains.at[core], gains.at[core], gain_rel.at[0], gain_rel.at[1], sibling)

    def relay_hidden(d):
        f = chip_from(d)
        block = hf.at[core, f]
        drain(block, s1_dir.at[f])
        send(block, block, s1_sem.at[1], s1_rel.at[0], sibling)

    plane_loop(relay_hidden)
    drain(hf.at[other], s1_rel.at[0])
    drain(gains.at[other], gain_rel.at[1])

    total = jnp.zeros((B, B), F32)
    for c in range(NC):
        for k in range(2):
            x = hf[k, c].astype(F32)
            total = total + x * x
    inv_rms = lax.rsqrt(jnp.sum(total, axis=1, keepdims=True) / float(D) + 1e-05)
    for c in range(NC):
        for k in range(2):
            x = hf[k, c].astype(F32)
            emb[:, (2 * c + k) * B : (2 * c + k + 1) * B] = (x * inv_rms * gains[k, c]).astype(BF16)
    rms_row = jnp.broadcast_to(inv_rms, (B, B)).T[0:1, :]
    scale = float(D) ** -0.5
    arguments[4].wait()
    scores_t = (
        lax.dot_general(emb[...], q_ref[...], (((1,), (1,)), ((), ())), preferred_element_type=F32) * scale
    )
    masked = jnp.where(listed_t, scores_t, -1e30)
    top = jnp.max(masked, axis=0, keepdims=True)
    weight = jnp.where(listed_t, jnp.exp(masked - top), 0.0)
    part = jnp.sum(weight, axis=0, keepdims=True)
    stat_s[0:1, :] = jnp.where(part > 0.0, top + jnp.log(part), -1e30)
    stat_s[1:2, :] = rms_row
    stat_r[z] = stat_s[...]

    def send_stat(d):
        send(stat_s, stat_r.at[z], st_sem.at[0], st_sem.at[1], {"passage": z_at(d)})

    z_loop(send_stat)

    scores = scores_t.T
    for g in range(16):
        rows = slice(8 * g, 8 * g + 8)
        local = cand_ref[rows, :] - z * B
        mine = (local >= 0) & (local < B)
        sp_s[g] = jnp.where(mine, lanes(scores[rows, :], jnp.clip(local, 0, B - 1)), 0.0)
    sp_r[z] = sp_s[z]

    def send_sparse(d):
        t = z_at(d)
        send(sp_s.at[t], sp_r.at[z], sp_sem.at[0], sp_sem.at[1], {"passage": t})

    z_loop(send_sparse)

    drain(xz.at[pl.ds(0, NZ - 1)], xz_sem.at[1])
    ez[core, chip] = xz[...].reshape(B, B).astype(BF16)

    def send_rows(d):
        t = chip_at(d)
        block = ez.at[core, chip]
        send(block, block, ez_sem.at[0], ez_dir.at[chip], {"query": 2 * t + core})

    own_rows = ez.at[core, chip]
    send(own_rows, own_rows, ez_sem.at[1], ez_rel.at[0], sibling)
    plane_loop(send_rows)

    drain(stat_r.at[pl.ds(0, NZ - 1)], st_sem.at[1])
    tops = [stat_r[k, 0:1, :] for k in range(NZ)]
    top_all = tops[0]
    for k in range(1, NZ):
        top_all = jnp.maximum(top_all, tops[k])
    norm = jnp.zeros((1, B), F32)
    for k in range(NZ):
        norm = norm + jnp.exp(tops[k] - top_all)
    table_t = jnp.where(listed_t, jnp.exp(masked - top_all) / norm - tgt_t[...], 0.0).astype(BF16)
    row_dot = jnp.sum(table_t.astype(F32) * scores_t, axis=1, keepdims=True)
    row_dot_row = jnp.broadcast_to(row_dot, (B, B)).T[0:1, :]
    for c in range(NC):
        both = jnp.dot(table_t, q_ref[:, c * 256 : (c + 1) * 256], preferred_element_type=F32)
        for k in range(2):
            e = both[:, k * B : (k + 1) * B]
            e32[k, c] = e
            eb[k, c] = e.astype(BF16)
            terms = e * hf[k, c].astype(F32) * inv_rms
            gs[2 * c + k, 0:1, :] = jnp.sum(terms, axis=0, keepdims=True)
            gs[2 * c + k, 1:2, :] = row_dot_row
    gm_r[me] = gs[me]

    def send_gain(d):
        for k in (core, other):
            t = 2 * chip_at(d) + k
            send(gs.at[t], gm_r.at[me], gm_sem.at[0], gm_sem.at[1], {"query": t})

    plane_loop(send_gain)
    send(gs.at[2 * chip + other], gm_r.at[me], gm_sem.at[0], gm_sem.at[1], sibling)
    send(eb.at[other], sib_r, sib_sem.at[0], sib_sem.at[1], sibling)

    drain(sp_r.at[pl.ds(0, NZ - 1)], sp_sem.at[1])
    logits = sp_r[0]
    for k in range(1, NZ):
        logits = logits + sp_r[k]
    w = jnp.exp(logits - jnp.max(logits, axis=1, keepdims=True))
    student = w / jnp.sum(w, axis=1, keepdims=True)
    my_rows = pl.ds(pl.multiple_of(z * 8, 8), 8)
    lg_s[...] = (student - tgt[my_rows, :]).astype(BF16).astype(F32)
    lg_r[z] = lg_s[...]

    def send_list(d):
        send(lg_s, lg_r.at[z], lg_sem.at[0], lg_sem.at[1], {"passage": z_at(d)})

    z_loop(send_list)

    drain(sib_r, sib_sem.at[1])
    for c in range(NC):
        s6_s[c] = (e32[core, c] + sib_r[c].astype(F32)).astype(BF16)
    s6_r[chip] = s6_s[chip]

    def send_grads(d):
        t = chip_at(d)
        send(s6_s.at[t], s6_r.at[chip], s6_sem.at[0], s6_sem.at[1], {"query": 2 * t + core})

    plane_loop(send_grads)

    half_inverse(1)
    for w in range(4):
        inv[w] = inv_t[w].T


    drain(gm_r.at[pl.ds(0, 31)], gm_sem.at[1])
    small = gm_r[0]
    for k in range(1, 32):
        small = small + gm_r[k]
    z7_s[...] = small[0:1, :]
    z7_r[z] = small[0:1, :]

    def send_plane_gain(d):
        send(z7_s, z7_r.at[z], z7_sem.at[0], z7_sem.at[1], {"passage": z_at(d)})

    z_loop(send_plane_gain)

    def relay_rows(d):
        f = chip_from(d)
        block = ez.at[core, f]
        drain(block, ez_dir.at[f])
        send(block, block, ez_sem.at[1], ez_rel.at[0], sibling)

    plane_loop(relay_rows)


    drain(ez.at[other], ez_rel.at[0])
    rms_rows = jnp.concatenate([stat_r[k, 1:2, :] for k in range(NZ)], axis=0)
    rms_t = jnp.concatenate([rms_rows, jnp.zeros((B - NZ, B), F32)], axis=0).T
    for c in range(NC):
        col = jnp.concatenate(
            [jnp.broadcast_to(rms_t[8 * c : 8 * c + 8, k : k + 1], (8, B)) for k in range(NZ)], axis=0
        )
        for k in range(2):
            raw = ez[k, c].astype(F32)
            embz[c * B : (c + 1) * B, k * B : (k + 1) * B] = (raw * col * gains[k, z]).astype(BF16)
    drain(lg_r.at[pl.ds(0, NZ - 1)], lg_sem.at[1])
    for g in range(0, 16, 2):
        for b in range(NC):
            cols = slice(b * B, (b + 1) * B)
            two = []
            for k in (g, g + 1):
                i = lax.shift_right_logical(inv[b // 4, 8 * k : 8 * k + 8, :], 8 * (b % 4))
                i = lax.bitwise_and(i, 255)
                two.append(jnp.where(i > 0, lanes(lg_r[k], jnp.maximum(i - 1, 0)), 0.0))
            gfull[8 * g : 8 * g + 16, cols] = jnp.concatenate(two, axis=0).astype(BF16)
    qg_ref[...] = jnp.dot(gfull[...], embz[...], preferred_element_type=F32).astype(BF16)

    drain(s6_r.at[pl.ds(0, NC - 1)], s6_sem.at[1])
    e_grad = s6_r[0].astype(F32)
    for c in range(1, NC):
        e_grad = e_grad + s6_r[c].astype(F32)
    dot_col = jnp.broadcast_to(small[1:2, :], (B, B)).T
    hg_ref[...] = (
        inv_rms * (e_grad * gain_row) - hid_ref[...].astype(F32) * (inv_rms * inv_rms) * (dot_col * scale)
    ).astype(BF16)

    drain(z7_r.at[pl.ds(0, NZ - 1)], z7_sem.at[1])
    gain_grad = z7_r[0]
    for k in range(1, NZ):
        gain_grad = gain_grad + z7_r[k]
    gg_ref[...] = gain_grad

    n = NC - 1
    drain(xp.at[pl.ds(0, n)], small_sem.at[0])
    drain(hf.at[0, pl.ds(0, n)], s1_sem.at[0])
    drain(hf.at[0], s1_sem.at[1])
    drain(gains.at[0, pl.ds(0, n)], gain_sem.at[0])
    drain(gains.at[0], gain_rel.at[0])
    drain(xz.at[pl.ds(0, n)], xz_sem.at[0])
    drain(stat_r.at[pl.ds(0, n)], st_sem.at[0])
    drain(sp_r.at[pl.ds(0, n)], sp_sem.at[0])
    drain(lg_r.at[pl.ds(0, n)], lg_sem.at[0])
    drain(ez.at[0, pl.ds(0, n)], ez_sem.at[0])
    drain(ez.at[0], ez_sem.at[1])
    drain(sib_r, sib_sem.at[0])
    drain(gm_r.at[pl.ds(0, 31)], gm_sem.at[0])
    drain(s6_r.at[pl.ds(0, n)], s6_sem.at[0])
    drain(z7_r.at[pl.ds(0, n)], z7_sem.at[0])


def shards(queries, cand_ids, teacher, hidden_states, gain):
    vmem = pl.BlockSpec(memory_space=pltpu.VMEM)
    two = pltpu.SemaphoreType.DMA((2,))
    arguments = (queries, cand_ids, teacher, hidden_states, gain.reshape(1, B))
    q_grad, h_grad, gain_grad = pl.pallas_call(
        kernel,
        name="listwise",
        out_shape=(
            jax.ShapeDtypeStruct((B, 2 * B), BF16),
            jax.ShapeDtypeStruct((B, B), BF16),
            jax.ShapeDtypeStruct((1, B), F32),
        ),
        in_specs=[pl.BlockSpec(memory_space=pltpu.HBM)] * 5,
        out_specs=(vmem, vmem, vmem),
        scratch_shapes=[
            pltpu.VMEM((B, D), BF16),
            pltpu.VMEM((B, B), I32),
            pltpu.VMEM((B, B), I32),
            pltpu.VMEM((B, B), BF16),
            pltpu.VMEM((1, B), BF16),
            pltpu.SemaphoreType.DMA((5,)),
            pltpu.VMEM((2, NC, B, B), BF16),
            pltpu.VMEM((2, NC, 1, B), F32),
            two,
            two,
            pltpu.VMEM((NC, 8, B), F32),
            pltpu.VMEM((NC, 8, B), F32),
            pltpu.VMEM((NZ, 8, B), F32),
            pltpu.VMEM((2, NC, B, B), BF16),
            pltpu.VMEM((B, D), BF16),
            pltpu.VMEM((B, B), I32),
            pltpu.VMEM((B, B), I32),
            pltpu.VMEM((4, B, B), I32),
            pltpu.VMEM((4, B, B), I32),
            pltpu.VMEM((4, B, B), I32),
            pltpu.VMEM((B, B), F32),
            pltpu.VMEM((B, B), F32),
            pltpu.VMEM((B, B), F32),
            pltpu.VMEM((2, B), F32),
            pltpu.VMEM((NZ, 2, B), F32),
            pltpu.VMEM((NZ, 8, B), F32),
            pltpu.VMEM((NZ, 8, B), F32),
            pltpu.VMEM((8, B), F32),
            pltpu.VMEM((NZ, 8, B), F32),
            pltpu.VMEM((B, NC * B), BF16),
            pltpu.VMEM((NC * B, 2 * B), BF16),
            pltpu.VMEM((2, NC, B, B), BF16),
            pltpu.VMEM((2, NC, B, B), F32),
            pltpu.VMEM((NC, B, B), BF16),
            pltpu.VMEM((32, 2, B), F32),
            pltpu.VMEM((32, 2, B), F32),
            pltpu.VMEM((NC, B, B), BF16),
            pltpu.VMEM((NC, B, B), BF16),
            pltpu.VMEM((1, B), F32),
            pltpu.VMEM((NZ, 1, B), F32),
            two,
            pltpu.SemaphoreType.DMA((NC,)),
            pltpu.SemaphoreType.DMA((1,)),
            two,
            two,
            two,
            two,
            two,
            two,
            pltpu.SemaphoreType.DMA((NC,)),
            pltpu.SemaphoreType.DMA((1,)),
            two,
            two,
            two,
            two,
            pltpu.SemaphoreType.REGULAR,
        ],
        compiler_params=pltpu.CompilerParams(
            collective_id=0, has_side_effects=True, vmem_limit_bytes=48 * 2**20
        ),
    )(*[pltpu.with_memory_space_constraint(x, pltpu.HBM) for x in arguments])
    return q_grad, h_grad, gain_grad.reshape(B)


def solution(mesh):
    placed = (
        P("query", None),
        P("query", None),
        P("query", None),
        P("passage", "query"),
        P("query"),
    )
    return jax.shard_map(
        shards,
        mesh=mesh,
        in_specs=placed,
        out_specs=(P("query", "passage"), P("passage", "query"), P("query")),
        check_vma=False,
    )
```

```python
import jax
import jax.numpy as jnp
from jax import lax
from jax.experimental import pallas as pl
from jax.experimental.pallas import tpu as pltpu
from jax.sharding import PartitionSpec as P

D = 4096
MESH = pl.DeviceIdType.MESH
F32, BF16, I32 = jnp.float32, jnp.bfloat16, jnp.int32
FAR_FIRST = (10, 6, 9, 11, 14, 2, 8, 5, 7, 13, 15, 1, 3, 4, 12)
NEAR_Z = (4, 12, 3, 13, 2, 14, 1, 15)
FAR_Z = (8, 7, 9, 6, 10, 5, 11, 4, 12, 3, 13, 2, 14, 1, 15)
NZ = 16
NC = 16
B = 128


def lanes(x, index):
    return jnp.take_along_axis(x, index, axis=1)


def kernel(
    q_hbm, cand_hbm, teach_hbm, hid_hbm, gain_hbm,
    qg_ref, hg_ref, gg_ref,
    q_ref, cand_ref, teach_ref, hid_ref, gain_ref, in_sem,
    hf, gains, gain_sem, gain_rel, hid32, xp, xz, ez, emb, cand_t, inv_at, inv_code, inv_t, inv, tgt, tgt_t, sg, stat_s, stat_r, sp_s, sp_r,
    lg_s, lg_r, gfull, embz, eb, e32, sib_r, gs, gm_r, s6_s, s6_r, z7_s, z7_r,
    s1_sem, s1_dir, s1_rel, small_sem, xz_sem, st_sem, sp_sem, lg_sem, ez_sem, ez_dir, ez_rel,
    sib_sem, gm_sem, s6_sem, z7_sem, far_sem,
):
    me = lax.axis_index("query")
    z = lax.axis_index("passage")
    core = lax.bitwise_and(me, 1)
    other = 1 - core
    chip = lax.shift_right_logical(me, 1)
    cy, cx = lax.shift_right_logical(chip, 2), lax.bitwise_and(chip, 3)
    sibling = {"query": 2 * chip + other}

    def chip_at(d):
        ty = lax.bitwise_and(cy + d // 4, 3)
        tx = lax.bitwise_and(cx + d, 3)
        return 4 * ty + tx

    def chip_from(d):
        return 4 * lax.bitwise_and(cy - d // 4 + 4, 3) + lax.bitwise_and(cx - d + NC, 3)

    def z_at(d):
        return lax.bitwise_and(z + d, NZ - 1)

    def plane_loop(body):
        for d in FAR_FIRST:
            body(d)

    def z_loop(body):
        for d in FAR_Z:
            body(d)

    def each(first, last, body):
        def step(d, carry):
            body(d)
            return carry

        lax.fori_loop(first, last, step, 0)

    def send(src, dst, s_sem, r_sem, where):
        pltpu.make_async_remote_copy(
            src_ref=src, dst_ref=dst, send_sem=s_sem, recv_sem=r_sem,
            device_id=where, device_id_type=MESH,
        ).start()

    def drain(ref, sem):
        pltpu.make_async_copy(ref, ref, sem).wait()

    arguments = [
        pltpu.make_async_copy(src, dst, in_sem.at[k])
        for k, (src, dst) in enumerate(
            [(hid_hbm, hid_ref), (gain_hbm, gain_ref), (cand_hbm, cand_ref), (teach_hbm, teach_ref), (q_hbm, q_ref)]
        )
    ]
    for argument in arguments:
        argument.start()

    barrier = pltpu.get_barrier_semaphore()

    def hail_z(d):
        pl.semaphore_signal(barrier, inc=1, device_id={"passage": z_at(d)}, device_id_type=MESH)

    def hail_plane(d):
        for k in (core, other):
            pl.semaphore_signal(barrier, inc=1, device_id={"query": 2 * chip_at(d) + k}, device_id_type=MESH)

    for d in NEAR_Z:
        hail_z(d)
    plane_loop(hail_plane)
    pl.semaphore_signal(barrier, inc=1, device_id=sibling, device_id_type=MESH)

    arguments[0].wait()
    arguments[1].wait()
    hid = hid_ref[...]
    gain_row = gain_ref[...].astype(F32)
    hf[core, chip] = hid
    gains[core, chip] = gain_row
    h32 = hid.astype(F32)
    hid32[...] = h32.reshape(NC, 8, B)
    xp[chip] = hid32[chip]

    arguments[2].wait()
    arguments[3].wait()
    t = teach_ref[...].astype(F32) * 0.125
    t = jnp.exp(t - jnp.max(t, axis=1, keepdims=True))
    tgt[...] = t / jnp.sum(t, axis=1, keepdims=True)

    cand_t[...] = cand_ref[...].T
    own_at = lax.broadcasted_iota(I32, (B, B), 0) + z * B

    def own_step(k, acc):
        for c in range(8):
            acc = jnp.where(cand_t[pl.ds(8 * k + c, 1), :] == own_at, 8 * k + c, acc)
        return acc

    inv_own_t = lax.fori_loop(0, B // 8, own_step, jnp.full((B, B), -1, I32))
    listed_t = inv_own_t >= 0
    inv_own = inv_own_t.T

    ids = cand_t[...]
    place = lax.bitwise_and(lax.shift_right_logical(ids, 3), NC - 1)
    inv_at[...] = lax.shift_left(lax.shift_right_logical(ids, 7), 3) + lax.bitwise_and(ids, 7)
    code = lax.shift_left(
        lax.broadcasted_iota(I32, (B, B), 0) + 1, 8 * lax.bitwise_and(place, 3)
    )
    for w in range(4):
        inv_code[w] = jnp.where(lax.shift_right_logical(place, 2) == w, code, 0)

    def half_inverse(h):
        half = B // 2
        at = lax.broadcasted_iota(I32, (half, B), 0) + half * h

        def step(k, accs):
            accs = list(accs)
            for u in range(8):
                row = pl.ds(8 * k + u, 1)
                hit = inv_at[row, :] == at
                for w in range(4):
                    accs[w] = lax.bitwise_or(jnp.where(hit, inv_code[w, row, :], 0), accs[w])
            return tuple(accs)

        accs = lax.fori_loop(0, B // 8, step, tuple(jnp.zeros((half, B), I32) for _ in range(4)))
        for w in range(4):
            inv_t[w, half * h : half * (h + 1), :] = accs[w]

    pl.semaphore_wait(barrier, 31 + len(NEAR_Z))
    for d in (4, 12):
        pl.semaphore_signal(far_sem, inc=1, device_id={"passage": z_at(d)}, device_id_type=MESH)

    def send_small(d):
        t = chip_at(d)
        send(hid32.at[t], xp.at[chip], small_sem.at[0], small_sem.at[1], {"query": 2 * t + core})

    def send_hidden(d):
        t = chip_at(d)
        block = hf.at[core, chip]
        send(block, block, s1_sem.at[0], s1_dir.at[chip], {"query": 2 * t + core})

    plane_loop(send_small)

    def send_own_gain(d):
        t = chip_at(d)
        row = gains.at[core, chip]
        send(row, row, gain_sem.at[0], gain_sem.at[1], {"query": 2 * t + core})

    plane_loop(send_own_gain)
    own = hf.at[core, chip]
    send(own, own, s1_sem.at[1], s1_rel.at[0], sibling)
    plane_loop(send_hidden)

    for g in range(16):
        rows = slice(8 * g, 8 * g + 8)
        i = inv_own[rows, :]
        sg[rows, :] = jnp.where(i >= 0, lanes(tgt[rows, :], jnp.maximum(i, 0)), 0.0)
    tgt_t[...] = sg[...].T
    half_inverse(0)

    pl.semaphore_wait(far_sem, 2)

    drain(xp.at[pl.ds(0, NC - 1)], small_sem.at[1])
    xz[z] = xp[z]

    def send_slice(d):
        t = z_at(d)
        send(xp.at[t], xz.at[z], xz_sem.at[0], xz_sem.at[1], {"passage": t})

    z_loop(send_slice)
    drain(gains.at[core, pl.ds(0, NC - 1)], gain_sem.at[1])
    send(gains.at[core], gains.at[core], gain_rel.at[0], gain_rel.at[1], sibling)

    def relay_hidden(d):
        f = chip_from(d)
        block = hf.at[core, f]
        drain(block, s1_dir.at[f])
        send(block, block, s1_sem.at[1], s1_rel.at[0], sibling)

    mine = hf[core, chip].astype(F32)
    total = mine * mine
    for d in FAR_FIRST:
        relay_hidden(d)
        block = hf[core, chip_from(d)].astype(F32)
        total = total + block * block
    drain(hf.at[other], s1_rel.at[0])
    drain(gains.at[other], gain_rel.at[1])

    for c in range(NC):
        block = hf[other, c].astype(F32)
        total = total + block * block
    inv_rms = lax.rsqrt(jnp.sum(total, axis=1, keepdims=True) / float(D) + 1e-05)
    for c in range(NC):
        for k in range(2):
            x = hf[k, c].astype(F32)
            emb[:, (2 * c + k) * B : (2 * c + k + 1) * B] = (x * inv_rms * gains[k, c]).astype(BF16)
    rms_row = jnp.broadcast_to(inv_rms, (B, B)).T[0:1, :]
    scale = float(D) ** -0.5
    arguments[4].wait()
    scores_t = (
        lax.dot_general(emb[...], q_ref[...], (((1,), (1,)), ((), ())), preferred_element_type=F32) * scale
    )
    masked = jnp.where(listed_t, scores_t, -1e30)
    top = jnp.max(masked, axis=0, keepdims=True)
    weight = jnp.where(listed_t, jnp.exp(masked - top), 0.0)
    part = jnp.sum(weight, axis=0, keepdims=True)
    stat_s[0:1, :] = jnp.where(part > 0.0, top + jnp.log(part), -1e30)
    stat_s[1:2, :] = rms_row
    stat_r[z] = stat_s[...]

    def send_stat(d):
        send(stat_s, stat_r.at[z], st_sem.at[0], st_sem.at[1], {"passage": z_at(d)})

    z_loop(send_stat)

    scores = scores_t.T
    for g in range(16):
        rows = slice(8 * g, 8 * g + 8)
        local = cand_ref[rows, :] - z * B
        mine = (local >= 0) & (local < B)
        sp_s[g] = jnp.where(mine, lanes(scores[rows, :], jnp.clip(local, 0, B - 1)), 0.0)
    sp_r[z] = sp_s[z]

    def send_sparse(d):
        t = z_at(d)
        send(sp_s.at[t], sp_r.at[z], sp_sem.at[0], sp_sem.at[1], {"passage": t})

    z_loop(send_sparse)

    drain(xz.at[pl.ds(0, NZ - 1)], xz_sem.at[1])
    ez[core, chip] = xz[...].reshape(B, B).astype(BF16)

    def send_rows(d):
        t = chip_at(d)
        block = ez.at[core, chip]
        send(block, block, ez_sem.at[0], ez_dir.at[chip], {"query": 2 * t + core})

    own_rows = ez.at[core, chip]
    send(own_rows, own_rows, ez_sem.at[1], ez_rel.at[0], sibling)
    plane_loop(send_rows)

    drain(stat_r.at[pl.ds(0, NZ - 1)], st_sem.at[1])
    tops = [stat_r[k, 0:1, :] for k in range(NZ)]
    top_all = tops[0]
    for k in range(1, NZ):
        top_all = jnp.maximum(top_all, tops[k])
    norm = jnp.zeros((1, B), F32)
    for k in range(NZ):
        norm = norm + jnp.exp(tops[k] - top_all)
    table_t = jnp.where(listed_t, jnp.exp(masked - top_all) / norm - tgt_t[...], 0.0).astype(BF16)
    row_dot = jnp.sum(table_t.astype(F32) * scores_t, axis=1, keepdims=True)
    row_dot_row = jnp.broadcast_to(row_dot, (B, B)).T[0:1, :]
    for c in range(NC):
        both = jnp.dot(table_t, q_ref[:, c * 256 : (c + 1) * 256], preferred_element_type=F32)
        for k in range(2):
            e = both[:, k * B : (k + 1) * B]
            e32[k, c] = e
            eb[k, c] = e.astype(BF16)
            terms = e * hf[k, c].astype(F32) * inv_rms
            gs[2 * c + k, 0:1, :] = jnp.sum(terms, axis=0, keepdims=True)
            gs[2 * c + k, 1:2, :] = row_dot_row
    gm_r[me] = gs[me]

    def send_gain(d):
        for k in (core, other):
            t = 2 * chip_at(d) + k
            send(gs.at[t], gm_r.at[me], gm_sem.at[0], gm_sem.at[1], {"query": t})

    plane_loop(send_gain)
    send(gs.at[2 * chip + other], gm_r.at[me], gm_sem.at[0], gm_sem.at[1], sibling)
    send(eb.at[other], sib_r, sib_sem.at[0], sib_sem.at[1], sibling)

    drain(sp_r.at[pl.ds(0, NZ - 1)], sp_sem.at[1])
    logits = sp_r[0]
    for k in range(1, NZ):
        logits = logits + sp_r[k]
    w = jnp.exp(logits - jnp.max(logits, axis=1, keepdims=True))
    student = w / jnp.sum(w, axis=1, keepdims=True)
    my_rows = pl.ds(pl.multiple_of(z * 8, 8), 8)
    lg_s[...] = (student - tgt[my_rows, :]).astype(BF16).astype(F32)
    lg_r[z] = lg_s[...]

    def send_list(d):
        send(lg_s, lg_r.at[z], lg_sem.at[0], lg_sem.at[1], {"passage": z_at(d)})

    z_loop(send_list)

    drain(sib_r, sib_sem.at[1])
    for c in range(NC):
        s6_s[c] = (e32[core, c] + sib_r[c].astype(F32)).astype(BF16)
    s6_r[chip] = s6_s[chip]

    def send_grads(d):
        t = chip_at(d)
        send(s6_s.at[t], s6_r.at[chip], s6_sem.at[0], s6_sem.at[1], {"query": 2 * t + core})

    plane_loop(send_grads)

    half_inverse(1)
    for w in range(4):
        inv[w] = inv_t[w].T


    drain(gm_r.at[pl.ds(0, 31)], gm_sem.at[1])
    small = gm_r[0]
    for k in range(1, 32):
        small = small + gm_r[k]
    z7_s[...] = small[0:1, :]
    z7_r[z] = small[0:1, :]

    def send_plane_gain(d):
        send(z7_s, z7_r.at[z], z7_sem.at[0], z7_sem.at[1], {"passage": z_at(d)})

    z_loop(send_plane_gain)

    def relay_rows(d):
        f = chip_from(d)
        block = ez.at[core, f]
        drain(block, ez_dir.at[f])
        send(block, block, ez_sem.at[1], ez_rel.at[0], sibling)

    plane_loop(relay_rows)


    drain(ez.at[other], ez_rel.at[0])
    rms_rows = jnp.concatenate([stat_r[k, 1:2, :] for k in range(NZ)], axis=0)
    rms_t = jnp.concatenate([rms_rows, jnp.zeros((B - NZ, B), F32)], axis=0).T
    for c in range(NC):
        col = jnp.concatenate(
            [jnp.broadcast_to(rms_t[8 * c : 8 * c + 8, k : k + 1], (8, B)) for k in range(NZ)], axis=0
        )
        for k in range(2):
            raw = ez[k, c].astype(F32)
            embz[c * B : (c + 1) * B, k * B : (k + 1) * B] = (raw * col * gains[k, z]).astype(BF16)
    drain(lg_r.at[pl.ds(0, NZ - 1)], lg_sem.at[1])
    for g in range(0, 16, 2):
        for b in range(NC):
            cols = slice(b * B, (b + 1) * B)
            two = []
            for k in (g, g + 1):
                i = lax.shift_right_logical(inv[b // 4, 8 * k : 8 * k + 8, :], 8 * (b % 4))
                i = lax.bitwise_and(i, 255)
                two.append(jnp.where(i > 0, lanes(lg_r[k], jnp.maximum(i - 1, 0)), 0.0))
            gfull[8 * g : 8 * g + 16, cols] = jnp.concatenate(two, axis=0).astype(BF16)
    qg_ref[...] = jnp.dot(gfull[...], embz[...], preferred_element_type=F32).astype(BF16)

    drain(s6_r.at[pl.ds(0, NC - 1)], s6_sem.at[1])
    e_grad = s6_r[0].astype(F32)
    for c in range(1, NC):
        e_grad = e_grad + s6_r[c].astype(F32)
    dot_col = jnp.broadcast_to(small[1:2, :], (B, B)).T
    hg_ref[...] = (
        inv_rms * (e_grad * gain_row) - hid_ref[...].astype(F32) * (inv_rms * inv_rms) * (dot_col * scale)
    ).astype(BF16)

    drain(z7_r.at[pl.ds(0, NZ - 1)], z7_sem.at[1])
    gain_grad = z7_r[0]
    for k in range(1, NZ):
        gain_grad = gain_grad + z7_r[k]
    gg_ref[...] = gain_grad

    n = NC - 1
    drain(xp.at[pl.ds(0, n)], small_sem.at[0])
    drain(hf.at[0, pl.ds(0, n)], s1_sem.at[0])
    drain(hf.at[0], s1_sem.at[1])
    drain(gains.at[0, pl.ds(0, n)], gain_sem.at[0])
    drain(gains.at[0], gain_rel.at[0])
    drain(xz.at[pl.ds(0, n)], xz_sem.at[0])
    drain(stat_r.at[pl.ds(0, n)], st_sem.at[0])
    drain(sp_r.at[pl.ds(0, n)], sp_sem.at[0])
    drain(lg_r.at[pl.ds(0, n)], lg_sem.at[0])
    drain(ez.at[0, pl.ds(0, n)], ez_sem.at[0])
    drain(ez.at[0], ez_sem.at[1])
    drain(sib_r, sib_sem.at[0])
    drain(gm_r.at[pl.ds(0, 31)], gm_sem.at[0])
    drain(s6_r.at[pl.ds(0, n)], s6_sem.at[0])
    drain(z7_r.at[pl.ds(0, n)], z7_sem.at[0])


def shards(queries, cand_ids, teacher, hidden_states, gain):
    vmem = pl.BlockSpec(memory_space=pltpu.VMEM)
    two = pltpu.SemaphoreType.DMA((2,))
    arguments = (queries, cand_ids, teacher, hidden_states, gain.reshape(1, B))
    q_grad, h_grad, gain_grad = pl.pallas_call(
        kernel,
        name="listwise",
        out_shape=(
            jax.ShapeDtypeStruct((B, 2 * B), BF16),
            jax.ShapeDtypeStruct((B, B), BF16),
            jax.ShapeDtypeStruct((1, B), F32),
        ),
        in_specs=[pl.BlockSpec(memory_space=pltpu.HBM)] * 5,
        out_specs=(vmem, vmem, vmem),
        scratch_shapes=[
            pltpu.VMEM((B, D), BF16),
            pltpu.VMEM((B, B), I32),
            pltpu.VMEM((B, B), I32),
            pltpu.VMEM((B, B), BF16),
            pltpu.VMEM((1, B), BF16),
            pltpu.SemaphoreType.DMA((5,)),
            pltpu.VMEM((2, NC, B, B), BF16),
            pltpu.VMEM((2, NC, 1, B), F32),
            two,
            two,
            pltpu.VMEM((NC, 8, B), F32),
            pltpu.VMEM((NC, 8, B), F32),
            pltpu.VMEM((NZ, 8, B), F32),
            pltpu.VMEM((2, NC, B, B), BF16),
            pltpu.VMEM((B, D), BF16),
            pltpu.VMEM((B, B), I32),
            pltpu.VMEM((B, B), I32),
            pltpu.VMEM((4, B, B), I32),
            pltpu.VMEM((4, B, B), I32),
            pltpu.VMEM((4, B, B), I32),
            pltpu.VMEM((B, B), F32),
            pltpu.VMEM((B, B), F32),
            pltpu.VMEM((B, B), F32),
            pltpu.VMEM((2, B), F32),
            pltpu.VMEM((NZ, 2, B), F32),
            pltpu.VMEM((NZ, 8, B), F32),
            pltpu.VMEM((NZ, 8, B), F32),
            pltpu.VMEM((8, B), F32),
            pltpu.VMEM((NZ, 8, B), F32),
            pltpu.VMEM((B, NC * B), BF16),
            pltpu.VMEM((NC * B, 2 * B), BF16),
            pltpu.VMEM((2, NC, B, B), BF16),
            pltpu.VMEM((2, NC, B, B), F32),
            pltpu.VMEM((NC, B, B), BF16),
            pltpu.VMEM((32, 2, B), F32),
            pltpu.VMEM((32, 2, B), F32),
            pltpu.VMEM((NC, B, B), BF16),
            pltpu.VMEM((NC, B, B), BF16),
            pltpu.VMEM((1, B), F32),
            pltpu.VMEM((NZ, 1, B), F32),
            two,
            pltpu.SemaphoreType.DMA((NC,)),
            pltpu.SemaphoreType.DMA((1,)),
            two,
            two,
            two,
            two,
            two,
            two,
            pltpu.SemaphoreType.DMA((NC,)),
            pltpu.SemaphoreType.DMA((1,)),
            two,
            two,
            two,
            two,
            pltpu.SemaphoreType.REGULAR,
        ],
        compiler_params=pltpu.CompilerParams(
            collective_id=0, has_side_effects=True, vmem_limit_bytes=48 * 2**20
        ),
    )(*[pltpu.with_memory_space_constraint(x, pltpu.HBM) for x in arguments])
    return q_grad, h_grad, gain_grad.reshape(B)


def solution(mesh):
    placed = (
        P("query", None),
        P("query", None),
        P("query", None),
        P("passage", "query"),
        P("query"),
    )
    return jax.shard_map(
        shards,
        mesh=mesh,
        in_specs=placed,
        out_specs=(P("query", "passage"), P("passage", "query"), P("query")),
        check_vma=False,
    )
```
